128 devices in a mesh: pose: 16 (over y_hi, z, core), text: 8 (over y_lo, x).
Axes of the slice: x: 4, y: 4 (y_hi: 2, y_lo: 2; y = y_hi * 2 + y_lo), z: 4, core: 2. Of those that a mesh axis runs over, the one named last changes fastest.
Arguments:
- pose_emb: float32 [16384, 768], P(('pose', 'text')), may hold values from -100 to 100
- text_emb: float32 [16384, 768], P(('pose', 'text')), may hold values from -6 to 6
- positive: int32 [16384], P(('pose', 'text')), may hold values from 0 to 16383, each once
Outputs:
- loss: float32 [], replicated
- pose_grad: float32 [16384, 768], P(('pose', 'text'))
- text_grad: float32 [16384, 768], P(('pose', 'text'))
The draws below stay inside these ranges and needn't reach their ends.
All inputs are finite; a program needn't handle non-finite values.
Results may differ from the reference program's by a relative error of at most 0.0003.
Values sent between devices are 32-bit elements; how exact they have to be, the bound alone decides.
A program may use at most 64 MiB of HBM per device.

```python
import math
import jax
import jax.numpy as jnp
from jax import lax

E = 768
N = 16384


def shared_texts(key):
    return jnp.clip(jax.random.normal(key, (N, E), jnp.float32), -6.0, 6.0)


def draw_text_emb(key, part):
    return shared_texts(key)


def drawn_rows(texts):
    strength = (60.0 + 120.0 * jnp.arange(16, dtype=jnp.float32) / 15.0) / jnp.sqrt(jnp.float32(E))
    aligned = strength[:, None] * (texts[0:32:2] + 0.98 * texts[1:32:2])
    return jnp.clip(aligned, -100.0, 100.0)


def draw_pose_emb(key, part):
    texts = shared_texts(key)
    key = jax.random.fold_in(key, 7)
    base = jnp.clip(jax.random.normal(key, (N, E), jnp.float32), -6.0, 6.0)
    return base.at[0:16].set(drawn_rows(texts))


def setup_inputs(seed: int = 0) -> dict:
    seeds = jax.random.split(jax.random.key(seed), 4)
    pose_emb = draw_pose_emb(jax.random.fold_in(seeds[3], 71), 0)
    text_emb = draw_text_emb(jax.random.fold_in(seeds[3], 71), 0)
    positive = jax.random.permutation(seeds[2], N).astype(jnp.int32)
    return {"pose_emb": pose_emb, "text_emb": text_emb, "positive": positive}


def logit_block(rows, cols, scale):
    return scale * jnp.dot(rows, cols.T, precision=lax.Precision.HIGHEST, preferred_element_type=jnp.float32)

def slope_block(logits, row_ids, col_ids, row_lse, col_lse):
    hit = (row_ids[:, None] == col_ids[None, :]).astype(jnp.float32)
    return 0.5 * (jnp.exp(logits - row_lse[:, None]) + jnp.exp(logits - col_lse[None, :])) - hit

def reference(pose_emb, text_emb, positive):
    total = pose_emb.shape[0]
    width = pose_emb.shape[1]
    scale = 2.0 / math.sqrt(width)
    step = math.gcd(total, 512)
    count = total // step
    col_ids = jnp.arange(total, dtype=jnp.int32)

    def first(carry, k):
        col_top, col_sum, matched = carry
        start = (k * step).astype(jnp.int32)
        part = lax.dynamic_slice_in_dim(pose_emb, start, step, 0)
        row_ids = lax.dynamic_slice_in_dim(positive, start, step, 0)
        logits = logit_block(part, text_emb, scale)
        row_top = lax.optimization_barrier(jnp.max(logits, axis=1))
        row_lse = row_top + jnp.log(lax.optimization_barrier(jnp.sum(jnp.exp(logits - row_top[:, None]), axis=1)))
        new_top = jnp.maximum(col_top, lax.optimization_barrier(jnp.max(logits, axis=0)))
        new_sum = col_sum * jnp.exp(col_top - new_top) + lax.optimization_barrier(jnp.sum(jnp.exp(logits - new_top[None, :]), axis=0))
        hit = row_ids[:, None] == col_ids[None, :]
        matched = matched + jnp.sum(jnp.where(hit, logits, jnp.float32(0.0)))
        return ((new_top, new_sum, matched), row_lse)
    init = (jnp.full((total,), -jnp.inf, jnp.float32), jnp.zeros((total,), jnp.float32), jnp.zeros((), jnp.float32))
    (col_top, col_sum, matched), row_lse = lax.scan(first, init, jnp.arange(count, dtype=jnp.int32))
    row_lse = row_lse.reshape(total)
    col_lse = col_top + jnp.log(col_sum)
    loss = (0.5 * (jnp.sum(row_lse) + jnp.sum(col_lse)) - matched) / total

    def second(acc, k):
        start = (k * step).astype(jnp.int32)
        part = lax.dynamic_slice_in_dim(pose_emb, start, step, 0)
        row_ids = lax.dynamic_slice_in_dim(positive, start, step, 0)
        lse_part = lax.dynamic_slice_in_dim(row_lse, start, step, 0)
        logits = logit_block(part, text_emb, scale)
        slope = slope_block(logits, row_ids, col_ids, lse_part, col_lse)
        pose_part = scale * jnp.dot(slope, text_emb, precision=lax.Precision.HIGHEST, preferred_element_type=jnp.float32)
        acc = acc + scale * lax.dot_general(slope, part, (((0,), (0,)), ((), ())), precision=lax.Precision.HIGHEST, preferred_element_type=jnp.float32)
        return (acc, pose_part)
    text_grad, pose_parts = lax.scan(second, jnp.zeros((total, width), jnp.float32), jnp.arange(count, dtype=jnp.int32))
    return (loss, pose_parts.reshape(total, width), text_grad)
```

```python
import functools
import math

import jax
import jax.numpy as jnp
from jax import lax
from jax.experimental import pallas as pl
from jax.experimental.pallas import tpu as pltpu
from jax.sharding import PartitionSpec as P

F32 = jnp.float32
BF16 = jnp.bfloat16
U = 128
H = U // 2


def split(v):
    hi = v.astype(BF16)
    return hi, (v - hi.astype(F32)).astype(BF16)


def dot_nt(a, b):
    return lax.dot_general(a, b, (((1,), (1,)), ((), ())), preferred_element_type=F32)


def dot_nn(a, b):
    return jnp.dot(a, b, preferred_element_type=F32)


def pick(k, values):
    out = values[-1]
    for i in range(len(values) - 2, -1, -1):
        out = jnp.where(k == i, values[i], out)
    return out


def loop(n, body):
    def step(i, carry):
        body(i)
        return carry

    lax.fori_loop(0, n, step, 0)


def kernel(
    scale,
    total,
    pose_ref,
    text_ref,
    pos_ref,
    loss_ref,
    pg_ref,
    tg_ref,
    xf,
    tf,
    xhl,
    xt,
    thl,
    lg,
    s_hi,
    s_lo,
    gp,
    gt,
    rp,
    rt,
    rsib,
    posbuf,
    rowst,
    colst,
    rowrec,
    colrec,
    la,
    lb,
    macc,
    ag_send,
    ag_recv,
    sib_send,
    sib_recv,
    pos_send,
    pos_recv,
    row_send,
    row_recv,
    col_send,
    col_recv,
    la_send,
    la_recv,
    lb_send,
    lb_recv,
    rs_send,
    rs_recv,
    rsib_send,
    rsib_recv,
):
    width = pose_ref.shape[1]
    pi = lax.axis_index("pose")
    ti = lax.axis_index("text")
    yhi, z, core = pi // 8, (pi // 2) % 4, pi % 2
    ylo, x = ti // 4, ti % 4

    def pabs(dy, dx):
        return (ylo + dy) % 2 * 4 + (x + dx) % 4

    def qabs(dy, dz):
        return (yhi + dy) % 2 * 4 + (z + dz) % 4

    def pose_peer(dy, dx):
        return (pi, pabs(dy, dx))

    def text_peer(dy, dz, dc=0):
        return (qabs(dy, dz) * 2 + (core + dc) % 2, (ylo + dy) % 2 * 4 + x)

    pose_peers = [(dy, dx) for dy in range(2) for dx in range(4) if (dy, dx) != (0, 0)]
    text_peers = [
        (dy, dz, dc)
        for dy in range(2)
        for dz in range(4)
        for dc in range(2)
        if (dy, dz, dc) != (0, 0, 0)
    ]

    barrier = pltpu.get_barrier_semaphore()
    for d in pose_peers:
        pl.semaphore_signal(barrier, inc=1, device_id=pose_peer(*d), device_id_type=pl.DeviceIdType.MESH)
    for d in text_peers:
        pl.semaphore_signal(barrier, inc=1, device_id=text_peer(*d), device_id_type=pl.DeviceIdType.MESH)
    me_p = pabs(0, 0)
    me_q = pi
    xf[me_p] = pose_ref[...]
    tf[me_q] = text_ref[...]
    posbuf[me_p] = jnp.broadcast_to(pos_ref[...], (8, U))
    pl.semaphore_wait(barrier, len(pose_peers) + len(text_peers))

    pending = []

    def copy(src, dst, ssem, rsem, dev):
        c = pltpu.make_async_remote_copy(
            src_ref=src,
            dst_ref=dst,
            send_sem=ssem,
            recv_sem=rsem,
            device_id=dev,
            device_id_type=pl.DeviceIdType.MESH,
        )
        c.start()
        pending.append(c)
        return c

    def await_recv(dst, rsem):
        pltpu.make_async_copy(dst, dst, rsem).wait()

    def buf(kind, dy, dd, h):
        if kind == 0:
            return xf.at[pabs(dy, dd), pl.ds(h * H, H)]
        return tf.at[qabs(dy, dd) * 2 + core, pl.ds(h * H, H)]

    def sib_buf(dy, dd, h, mine):
        c = core if mine else 1 - core
        return tf.at[qabs(dy, dd) * 2 + c, pl.ds(h * H, H)]

    def peer(kind, dy, dd):
        return pose_peer(dy, dd) if kind == 0 else text_peer(dy, dd, 0)

    send_count = [0, 0]

    def send(kind, src, h, to, arrives):
        n = send_count[kind]
        send_count[kind] += 1
        b = buf(kind, *src, h)
        copy(b, b, ag_send.at[kind, n], ag_recv.at[kind, (arrives[0] * 4 + arrives[1]) * 2 + h], peer(kind, *to))

    def got(kind, slot, h):
        await_recv(buf(kind, *slot, h), ag_recv.at[kind, (slot[0] * 4 + slot[1]) * 2 + h])
        if kind == 1:
            share(slot, h)

    def share(slot, h):
        i = (slot[0] * 4 + slot[1]) * 2 + h
        b = sib_buf(*slot, h, True)
        copy(b, b, sib_send.at[i], sib_recv.at[i], text_peer(0, 0, 1))

    def got_sib(slot):
        for h in range(2):
            i = (slot[0] * 4 + slot[1]) * 2 + h
            await_recv(sib_buf(*slot, h, False), sib_recv.at[i])

    NXT, PRV, PAR = (0, 1), (0, 3), (1, 0)
    for h in range(2):
        for kind in range(2):
            send(kind, (0, 0), h, NXT, (0, 3))
            send(kind, (0, 0), h, PRV, (0, 1))
            send(kind, (0, 0), h, PAR, (1, 0))
        share((0, 0), h)
    for n, d in enumerate(pose_peers):
        b = posbuf.at[me_p]
        copy(b, b, pos_send.at[n], pos_recv.at[(-d[0]) % 2 * 4 + (-d[1]) % 4], pose_peer(*d))

    def convert_pose(slot):
        a = pabs(*slot)
        v = xf[a]
        hi, lo = split(v)
        rows = pl.ds(pl.multiple_of(a * U, U), U)
        xhl[0, rows, :] = hi
        xhl[1, rows, :] = lo
        vt = v.T
        hi, lo = split(vt)
        xt[0, :, rows] = hi
        xt[1, :, rows] = lo

    def convert_text(slot):
        q = qabs(*slot)
        for c in range(2):
            hi, lo = split(tf[q * 2 + c])
            rows = pl.ds(pl.multiple_of((q * 2 + c) * U, U), U)
            thl[0, rows, :] = hi
            thl[1, rows, :] = lo

    def tile(rows, q):
        cols = pl.ds(pl.multiple_of(q * 2 * U, 2 * U), 2 * U)
        xh, xl = xhl[0, rows, :], xhl[1, rows, :]
        th, tl = thl[0, cols, :], thl[1, cols, :]
        lg[rows, cols] = scale * (dot_nt(xh, th) + dot_nt(xh, tl) + dot_nt(xl, th))

    def unit_rows(a):
        return pl.ds(pl.multiple_of(a * U, U), U)

    def block(pose_slots, text_slots):
        pa = [pabs(*s) for s in pose_slots]
        qa = [qabs(*s) for s in text_slots]

        def body(i):
            a = pick(i // len(qa), pa)
            tile(unit_rows(a), pick(i % len(qa), qa))

        loop(len(pa) * len(qa), body)

    for kind in range(2):
        got(kind, (0, 3), 0)
        send(kind, (0, 3), 0, NXT, (0, 2))
        got(kind, (1, 0), 0)
        send(kind, (1, 0), 0, NXT, (1, 3))
        send(kind, (1, 0), 0, PRV, (1, 1))
        got(kind, (0, 1), 0)
    convert_pose((0, 0))
    for kind in range(2):
        got(kind, (0, 1), 1)
        send(kind, (0, 1), 1, PRV, (0, 2))
        got(kind, (1, 0), 1)
        send(kind, (1, 0), 1, NXT, (1, 3))
        send(kind, (1, 0), 1, PRV, (1, 1))
        got(kind, (0, 3), 1)
    near = [(0, 0), (0, 3), (0, 1), (1, 0)]
    for s in near[1:]:
        convert_pose(s)
    for s in near:
        got_sib(s)
        convert_text(s)
    block(near, near)
    far = (0, 2)
    for kind in range(2):
        for h in range(2):
            got(kind, far, h)
            send(kind, far, h, PAR, (1, 2))
    convert_pose(far)
    got_sib(far)
    convert_text(far)
    block([far], near + [far])
    block(near, [far])
    last = [(1, 3), (1, 1), (1, 2)]
    for s in last:
        for kind in range(2):
            for h in range(2):
                got(kind, s, h)
        convert_pose(s)
    block(last, near + [far])
    for s in last:
        got_sib(s)
        convert_text(s)
    qs = [qabs(*s) for s in last]

    def all_rows(i):
        tile(pl.ds(pl.multiple_of((i // 3) * 256, 256), 256), pick(i % 3, qs))

    loop(12, all_rows)

    nt = 2 * 8

    def row_stats(a):
        rows = unit_rows(a)
        top = lg[rows, 0:U]
        for j in range(1, nt):
            top = jnp.maximum(top, lg[rows, j * U : (j + 1) * U])
        m = jnp.max(top, axis=1, keepdims=True)
        acc = jnp.exp(lg[rows, 0:U] - m)
        for j in range(1, nt):
            acc = acc + jnp.exp(lg[rows, j * U : (j + 1) * U] - m)
        mt = jnp.max(top.T, axis=0, keepdims=True)
        st = jnp.sum(acc.T, axis=0, keepdims=True)
        rowst[pl.ds(a, 1), :] = mt + jnp.log(st)

    loop(8, row_stats)

    def col_stats(b):
        cols = unit_rows(b)
        v = lg[:, cols]
        m = jnp.max(v, axis=0, keepdims=True)
        s = jnp.sum(jnp.exp(v - m), axis=0, keepdims=True)
        colst[pl.ds(b, 1), :] = m + jnp.log(s)

    loop(nt, col_stats)

    for n, d in enumerate(pose_peers):
        copy(rowst, rowrec.at[me_p], row_send.at[n], row_recv.at[(-d[0]) % 2 * 4 + (-d[1]) % 4], pose_peer(*d))
    for n, d in enumerate(text_peers):
        copy(
            colst,
            colrec.at[me_q],
            col_send.at[n],
            col_recv.at[((-d[0]) % 2 * 4 + (-d[1]) % 4) * 2 + d[2]],
            text_peer(*d),
        )
    rowrec[me_p] = rowst[...]
    colrec[me_q] = colst[...]
    for d in pose_peers:
        await_recv(posbuf.at[pabs(*d)], pos_recv.at[d[0] * 4 + d[1]])
    for d in pose_peers:
        await_recv(rowrec.at[pabs(*d)], row_recv.at[d[0] * 4 + d[1]])
    for d in text_peers:
        a = qabs(d[0], d[1]) * 2 + (core + d[2]) % 2
        await_recv(colrec.at[a], col_recv.at[(d[0] * 4 + d[1]) * 2 + d[2]])

    def lse_of(ref, n):
        m = ref[0]
        for j in range(1, n):
            m = jnp.maximum(m, ref[j])
        s = jnp.exp(ref[0] - m)
        for j in range(1, n):
            s = s + jnp.exp(ref[j] - m)
        return m + jnp.log(s)

    row_lse = lse_of(rowrec, 8)
    col_lse = lse_of(colrec, 16)
    rowst2 = rowrec.at[8]
    colst2 = colrec.at[16]
    rowst2[...] = row_lse
    colst2[...] = col_lse

    macc[...] = jnp.zeros_like(macc)

    def slope(a):
        rows = unit_rows(a)
        rl = jnp.broadcast_to(rowst2[pl.ds(a, 1), :], (U, U)).T
        ids = jnp.broadcast_to(posbuf[a][0:1, :].astype(F32), (U, U)).T
        lane = lax.broadcasted_iota(jnp.int32, (1, U), 1)
        acc = jnp.zeros((U, U), F32)
        for j in range(nt):
            cols = slice(j * U, (j + 1) * U)
            v = lg[rows, cols]
            cl = colst2[j : j + 1, :]
            yh = j // 8
            tt = (yhi + ylo + yh) % 2 * 4 + x
            base = (j * 8 + tt) * U
            hit = ids == (base + lane).astype(F32)
            p = 0.5 * (jnp.exp(v - rl) + jnp.exp(v - cl))
            acc = acc + jnp.where(hit, v, 0.0)
            hi, lo = split(jnp.where(hit, p - 1.0, p))
            s_hi[rows, cols] = hi
            s_lo[rows, cols] = lo
        t = acc[0:8]
        for k in range(1, U // 8):
            t = t + acc[k * 8 : (k + 1) * 8]
        macc[...] += t

    loop(8, slope)

    own = 0.5 * (rowst2[pl.ds(me_p, 1), :] + colst2[pl.ds(me_q, 1), :])
    first = lax.broadcasted_iota(jnp.int32, (8, U), 0) == 0
    la[me_p] = jnp.where(first, jnp.broadcast_to(own, (8, U)), 0.0) - macc[...]
    for n, d in enumerate(pose_peers):
        b = la.at[me_p]
        copy(b, b, la_send.at[n], la_recv.at[(-d[0]) % 2 * 4 + (-d[1]) % 4], pose_peer(*d))

    def pose_unit(slot):
        a = pabs(*slot)
        rows = unit_rows(a)
        sh, sl = s_hi[rows, :], s_lo[rows, :]
        gp[a] = dot_nn(sh, thl[0]) + dot_nn(sh, thl[1]) + dot_nn(sl, thl[0])

    def text_pair(slot):
        q = qabs(*slot)
        cols = pl.ds(pl.multiple_of(q * 2 * U, 2 * U), 2 * U)
        sh, sl = s_hi[:, cols], s_lo[:, cols]
        g = dot_nn(xt[0], sh) + dot_nn(xt[0], sl) + dot_nn(xt[1], sh)
        gt[q * 2] = g[:, 0:U]
        gt[q * 2 + 1] = g[:, U : 2 * U]
        i = slot[0] * 4 + slot[1]
        copy(gt.at[q * 2 + 1 - core], rsib.at[i], rsib_send.at[i], rsib_recv.at[i], text_peer(0, 0, 1))

    def g_at(kind, slot):
        if kind == 0:
            return gp.at[pabs(*slot)]
        return gt.at[qabs(*slot) * 2 + core]

    def r_at(kind, i):
        return (rp if kind == 0 else rt).at[i]

    def half(ref, h):
        n = ref.shape[0] // 2
        return ref.at[pl.ds(h * n, n)]

    rs_count = [0, 0]
    def rs_send_to(kind, slot, h, to, i):
        n = rs_count[kind]
        rs_count[kind] += 1
        copy(
            half(g_at(kind, slot), h),
            half(r_at(kind, i), h),
            rs_send.at[kind, n],
            rs_recv.at[kind, i * 2 + h],
            peer(kind, *to),
        )

    def rs_add(kind, slot, i, h):
        await_recv(half(r_at(kind, i), h), rs_recv.at[kind, i * 2 + h])
        dst, src = half(g_at(kind, slot), h), half(r_at(kind, i), h)
        dst[...] += src[...]

    def sib_add(slot):
        i = slot[0] * 4 + slot[1]
        await_recv(rsib.at[i], rsib_recv.at[i])
        dst = g_at(1, slot)
        dst[...] += rsib[i]

    def stage_a(kind):
        for h in range(2):
            rs_send_to(kind, (1, 2), h, PAR, 0)

    def stage_b(kind):
        for h in range(2):
            rs_send_to(kind, (1, 1), h, NXT, 1)
            rs_send_to(kind, (1, 3), h, PRV, 2)

    def stage_c(kind):
        rs_add(kind, (0, 2), 0, 0)
        rs_send_to(kind, (0, 2), 0, PRV, 3)
        rs_add(kind, (0, 2), 0, 1)
        rs_send_to(kind, (0, 2), 1, NXT, 3)

    def stage_d(kind):
        for h in range(2):
            rs_add(kind, (1, 0), 1, h)
            rs_add(kind, (1, 0), 2, h)
            rs_send_to(kind, (1, 0), h, PAR, 4)

    def stage_e(kind):
        rs_send_to(kind, (0, 3), 1, PRV, 5)
        rs_send_to(kind, (0, 1), 0, NXT, 6)
        rs_add(kind, (0, 3), 3, 0)
        rs_send_to(kind, (0, 3), 0, PRV, 5)
        rs_add(kind, (0, 1), 3, 1)
        rs_send_to(kind, (0, 1), 1, NXT, 6)

    pose_unit((1, 2))
    stage_a(0)
    text_pair((1, 2))
    pose_unit((1, 1))
    pose_unit((1, 3))
    stage_b(0)
    sib_add((1, 2))
    stage_a(1)
    text_pair((1, 1))
    text_pair((1, 3))
    pose_unit((0, 2))
    stage_c(0)
    sib_add((1, 1))
    sib_add((1, 3))
    stage_b(1)

    for d in pose_peers:
        await_recv(la.at[pabs(*d)], la_recv.at[d[0] * 4 + d[1]])
    t = la[0]
    for j in range(1, 8):
        t = t + la[j]
    lb[me_q] = t
    for n, d in enumerate(text_peers):
        b = lb.at[me_q]
        copy(
            b,
            b,
            lb_send.at[n],
            lb_recv.at[((-d[0]) % 2 * 4 + (-d[1]) % 4) * 2 + d[2]],
            text_peer(*d),
        )

    text_pair((0, 2))
    pose_unit((1, 0))
    stage_d(0)
    sib_add((0, 2))
    stage_c(1)
    text_pair((1, 0))
    pose_unit((0, 1))
    pose_unit((0, 3))
    stage_e(0)
    sib_add((1, 0))
    stage_d(1)
    text_pair((0, 1))
    text_pair((0, 3))
    pose_unit((0, 0))
    sib_add((0, 1))
    sib_add((0, 3))
    stage_e(1)
    text_pair((0, 0))
    sib_add((0, 0))

    for d in text_peers:
        a = qabs(d[0], d[1]) * 2 + (core + d[2]) % 2
        await_recv(lb.at[a], lb_recv.at[(d[0] * 4 + d[1]) * 2 + d[2]])
    t = lb[0]
    for j in range(1, 16):
        t = t + lb[j]
    loss_ref[0, 0] = jnp.sum(t) / total

    for h in range(2):
        for i in (4, 5, 6):
            rs_add(0, (0, 0), i, h)
    pg_ref[...] = scale * gp[me_p]
    for h in range(2):
        for i in (4, 5, 6):
            rs_add(1, (0, 0), i, h)
    tg_ref[...] = (scale * gt[me_q]).T

    for c in pending:
        c.wait_send()


def per_device(pose_emb, text_emb, positive):
    rows, width = pose_emb.shape
    total = rows * lax.axis_size("pose") * lax.axis_size("text")
    scale = 2.0 / math.sqrt(width)
    dma = pltpu.SemaphoreType.DMA
    vmem = pltpu.VMEM
    full = pl.BlockSpec(memory_space=pltpu.VMEM)
    loss, pose_grad, text_grad = pl.pallas_call(
        functools.partial(kernel, scale, total),
        out_shape=(
            jax.ShapeDtypeStruct((1, 1), F32),
            jax.ShapeDtypeStruct((rows, width), F32),
            jax.ShapeDtypeStruct((rows, width), F32),
        ),
        in_specs=[full] * 3,
        out_specs=(pl.BlockSpec(memory_space=pltpu.SMEM), full, full),
        scratch_shapes=[
            vmem((8, U, width), F32),
            vmem((16, U, width), F32),
            vmem((2, 8 * U, width), BF16),
            vmem((2, width, 8 * U), BF16),
            vmem((2, 16 * U, width), BF16),
            vmem((8 * U, 16 * U), F32),
            vmem((8 * U, 16 * U), BF16),
            vmem((8 * U, 16 * U), BF16),
            vmem((8, U, width), F32),
            vmem((16, width, U), F32),
            vmem((7, U, width), F32),
            vmem((7, width, U), F32),
            vmem((8, width, U), F32),
            vmem((8, 8, U), jnp.int32),
            vmem((8, U), F32),
            vmem((16, U), F32),
            vmem((9, 8, U), F32),
            vmem((17, 16, U), F32),
            vmem((8, 8, U), F32),
            vmem((16, 8, U), F32),
            vmem((8, U), F32),
            dma((2, 16)),
            dma((2, 16)),
            dma((16,)),
            dma((16,)),
            dma((8,)),
            dma((8,)),
            dma((8,)),
            dma((8,)),
            dma((16,)),
            dma((16,)),
            dma((8,)),
            dma((8,)),
            dma((16,)),
            dma((16,)),
            dma((2, 16)),
            dma((2, 16)),
            dma((8,)),
            dma((8,)),
        ],
        compiler_params=pltpu.CompilerParams(
            collective_id=0, has_side_effects=True, vmem_limit_bytes=64 * 1024 * 1024 - 64 * 1024
        ),
    )(pose_emb, text_emb, positive.reshape(1, rows))
    return (loss.reshape(()), pose_grad, text_grad)


def solution(mesh):
    return jax.shard_map(
        per_device,
        mesh=mesh,
        in_specs=(P(("pose", "text"), None), P(("pose", "text"), None), P(("pose", "text"))),
        out_specs=(P(), P(("pose", "text"), None), P(("pose", "text"), None)),
        check_vma=False,
    )
```

```python
import functools
import math

import jax
import jax.numpy as jnp
from jax import lax
from jax.experimental import pallas as pl
from jax.experimental.pallas import tpu as pltpu
from jax.sharding import PartitionSpec as P

F32 = jnp.float32
BF16 = jnp.bfloat16
U = 128
H = U // 2
LOG2E = math.log2(math.e)


def split(v):
    hi = v.astype(BF16)
    return hi, (v - hi.astype(F32)).astype(BF16)


def dot_nn(a, b):
    return jnp.dot(a, b, preferred_element_type=F32)


ORDER = [(0, 0), (0, 3), (0, 1), (1, 0), (0, 2), (1, 3), (1, 1), (1, 2)]
SLOT = {place: k for k, place in enumerate(ORDER)}
NXT, PRV, PAR = (0, 1), (0, 3), (1, 0)


def kernel(
    scale,
    total,
    pose_ref,
    text_ref,
    pos_ref,
    loss_ref,
    pg_ref,
    tg_ref,
    xf,
    tf,
    xhl,
    xt,
    thl,
    lg,
    sl,
    gp,
    gt,
    rp,
    rt,
    rsib,
    rm,
    rs,
    cm,
    cs,
    rlt,
    idt,
    rowst,
    colst,
    rowrec,
    colrec,
    la,
    lb,
    macc,
    ag_send,
    ag_recv,
    sib_send,
    sib_recv,
    row_send,
    row_recv,
    col_send,
    col_recv,
    la_send,
    la_recv,
    lb_send,
    lb_recv,
    rs_send,
    rs_recv,
    rsib_send,
    rsib_recv,
):
    width = pose_ref.shape[1]
    pi = lax.axis_index("pose")
    ti = lax.axis_index("text")
    yhi, z, core = pi // 8, (pi // 2) % 4, pi % 2
    ylo, x = ti // 4, ti % 4

    def pabs(dy, dx):
        return (ylo + dy) % 2 * 4 + (x + dx) % 4

    def qabs(dy, dz):
        return (yhi + dy) % 2 * 4 + (z + dz) % 4

    def pose_peer(dy, dx):
        return (pi, pabs(dy, dx))

    def text_peer(dy, dz, dc=0):
        return (qabs(dy, dz) * 2 + (core + dc) % 2, (ylo + dy) % 2 * 4 + x)

    pose_peers = [(dy, dx) for dy in range(2) for dx in range(4) if (dy, dx) != (0, 0)]
    text_peers = [
        (dy, dz, dc)
        for dy in range(2)
        for dz in range(4)
        for dc in range(2)
        if (dy, dz, dc) != (0, 0, 0)
    ]

    barrier = pltpu.get_barrier_semaphore()
    near_by = [pose_peer(*d) for d in (NXT, PRV, PAR)]
    near_by += [text_peer(*d) for d in (NXT, PRV, PAR)] + [text_peer(0, 0, 1)]
    for d in near_by:
        pl.semaphore_signal(barrier, inc=1, device_id=d, device_id_type=pl.DeviceIdType.MESH)
    me_p = pabs(0, 0)
    me_q = pi
    xf[me_p] = pose_ref[...]
    tf[me_q] = text_ref[...]
    pl.semaphore_wait(barrier, len(near_by))

    pending = []

    def copy(src, dst, ssem, rsem, dev):
        c = pltpu.make_async_remote_copy(
            src_ref=src,
            dst_ref=dst,
            send_sem=ssem,
            recv_sem=rsem,
            device_id=dev,
            device_id_type=pl.DeviceIdType.MESH,
        )
        c.start()
        pending.append(c)
        return c

    def await_recv(dst, rsem):
        pltpu.make_async_copy(dst, dst, rsem).wait()

    def buf(kind, dy, dd, h):
        if kind == 0:
            return xf.at[pabs(dy, dd), pl.ds(h * H, H)]
        return tf.at[qabs(dy, dd) * 2 + core, pl.ds(h * H, H)]

    def sib_buf(dy, dd, h, mine):
        c = core if mine else 1 - core
        return tf.at[qabs(dy, dd) * 2 + c, pl.ds(h * H, H)]

    def peer(kind, dy, dd):
        return pose_peer(dy, dd) if kind == 0 else text_peer(dy, dd, 0)

    send_count = [0, 0]

    def send(kind, src, h, to, arrives):
        n = send_count[kind]
        send_count[kind] += 1
        b = buf(kind, *src, h)
        copy(b, b, ag_send.at[kind, n], ag_recv.at[kind, SLOT[arrives] * 2 + h], peer(kind, *to))

    def got(kind, place, h):
        await_recv(buf(kind, *place, h), ag_recv.at[kind, SLOT[place] * 2 + h])
        if kind == 1:
            share(place, h)

    def share(place, h):
        i = SLOT[place] * 2 + h
        b = sib_buf(*place, h, True)
        copy(b, b, sib_send.at[i], sib_recv.at[i], text_peer(0, 0, 1))

    def got_sib(place):
        for h in range(2):
            i = SLOT[place] * 2 + h
            await_recv(sib_buf(*place, h, False), sib_recv.at[i])

    def rows_of(i, n=1):
        return slice(i * U, (i + n) * U)

    def cols_of(j, n=1):
        return slice(j * 2 * U, (j + n) * 2 * U)

    def convert_pose(i):
        v = xf[pabs(*ORDER[i])]
        xhl[0, rows_of(i), :], xhl[1, rows_of(i), :] = split(v)
        xt[0, :, rows_of(i)], xt[1, :, rows_of(i)] = split(v.T)

    def convert_text(j, dc):
        v = tf[qabs(*ORDER[j]) * 2 + (core + dc) % 2]
        rows = rows_of(2 * j + dc)
        thl[0, rows, :], thl[1, rows, :] = split(v)
        sl[0, 0:width, rows], sl[1, 0:width, rows] = split(v.T)

    seen_row, seen_col = set(), set()

    def stats(i, j):
        v = lg[rows_of(i), cols_of(j)]
        a, b = v[:, 0:U], v[:, U:]
        top = jnp.maximum(a, b)
        if i in seen_row:
            old = rm[i]
            top = jnp.maximum(top, old)
            rs[i] = rs[i] * jnp.exp2(old - top) + jnp.exp2(a - top) + jnp.exp2(b - top)
        else:
            rs[i] = jnp.exp2(a - top) + jnp.exp2(b - top)
        rm[i] = top
        w = v.reshape(U // 8, 8, 2 * U)
        top = jnp.max(w, axis=0)
        if j in seen_col:
            old = cm[:, cols_of(j)]
            top = jnp.maximum(top, old)
            cs[:, cols_of(j)] = cs[:, cols_of(j)] * jnp.exp2(old - top) + jnp.sum(jnp.exp2(w - top[None]), axis=0)
        else:
            cs[:, cols_of(j)] = jnp.sum(jnp.exp2(w - top[None]), axis=0)
        cm[:, cols_of(j)] = top
        seen_row.add(i)
        seen_col.add(j)

    waiting = []

    def logits(i, n, j):
        r, c = rows_of(i, n), cols_of(j)
        xh, xl = xhl[0, r, :], xhl[1, r, :]
        th, tl = sl[0, 0:width, c], sl[1, 0:width, c]
        value = (scale * LOG2E) * (dot_nn(xh, th) + dot_nn(xl, th) + dot_nn(xh, tl))
        flush()
        lg[r, c] = value
        waiting.extend((k, j) for k in range(i, i + n))

    def flush():
        for k, j in waiting:
            stats(k, j)
        waiting.clear()

    for h in range(2):
        for kind in range(2):
            send(kind, (0, 0), h, NXT, (0, 3))
            send(kind, (0, 0), h, PRV, (0, 1))
            send(kind, (0, 0), h, PAR, (1, 0))
        share((0, 0), h)
    convert_pose(0)
    convert_text(0, 0)

    for kind in range(2):
        got(kind, (0, 3), 0)
        send(kind, (0, 3), 0, NXT, (0, 2))
        got(kind, (1, 0), 0)
        send(kind, (1, 0), 0, PRV, (1, 1))
        got(kind, (0, 1), 0)
    for kind in range(2):
        send(kind, (1, 0), 0, NXT, (1, 3))
    got_sib((0, 0))
    convert_text(0, 1)
    for kind in range(2):
        got(kind, (0, 1), 1)
        send(kind, (0, 1), 1, PRV, (0, 2))
    for kind in range(2):
        got(kind, (1, 0), 1)
        send(kind, (1, 0), 1, NXT, (1, 3))
        send(kind, (1, 0), 1, PRV, (1, 1))
        got(kind, (0, 3), 1)
    for i in (1, 2, 3):
        convert_pose(i)
        convert_text(i, 0)
    for j in (1, 2, 3):
        got_sib(ORDER[j])
        convert_text(j, 1)
    for j in range(4):
        logits(0, 4, j)
    for h in range(2):
        for kind in range(2):
            got(kind, (0, 2), h)
            send(kind, (0, 2), h, PAR, (1, 2))
    convert_pose(4)
    convert_text(4, 0)
    got_sib((0, 2))
    convert_text(4, 1)
    for j in range(4):
        logits(4, 1, j)
    logits(0, 5, 4)
    flush()
    for i in (5, 6):
        for h in range(2):
            got(0, ORDER[i], h)
        convert_pose(i)
    for i in (5, 6):
        for h in range(2):
            got(1, ORDER[i], h)
        convert_text(i, 0)
    for j in range(5):
        logits(5, 2, j)
    for j in (5, 6):
        got_sib(ORDER[j])
        convert_text(j, 1)
        logits(0, 7, j)
    for kind in range(2):
        for h in range(2):
            got(kind, (1, 2), h)
    convert_pose(7)
    convert_text(7, 0)
    for j in range(7):
        logits(7, 1, j)
    got_sib((1, 2))
    convert_text(7, 1)
    logits(0, 8, 7)
    flush()

    for i in range(8):
        mt, st = rm[i].T, rs[i].T
        m = jnp.max(mt, axis=0, keepdims=True)
        s = jnp.sum(st * jnp.exp2(mt - m), axis=0, keepdims=True)
        rowst[pl.ds(pabs(*ORDER[i]), 1), :] = m + jnp.log2(s)
    rowst[8:16, :] = jnp.broadcast_to(pos_ref[...].astype(F32), (8, U))
    m = jnp.max(cm[...], axis=0, keepdims=True)
    s = jnp.sum(cs[...] * jnp.exp2(cm[...] - m), axis=0, keepdims=True)
    lse = m + jnp.log2(s)
    for j in range(8):
        for dc in range(2):
            p = qabs(*ORDER[j]) * 2 + (core + dc) % 2
            colst[pl.ds(p, 1), :] = lse[:, rows_of(2 * j + dc)]

    for n, d in enumerate(pose_peers):
        copy(rowst, rowrec.at[me_p], row_send.at[n], row_recv.at[(-d[0]) % 2 * 4 + (-d[1]) % 4], pose_peer(*d))
    for n, d in enumerate(text_peers):
        copy(
            colst,
            colrec.at[me_q],
            col_send.at[n],
            col_recv.at[((-d[0]) % 2 * 4 + (-d[1]) % 4) * 2 + d[2]],
            text_peer(*d),
        )
    rowrec[me_p] = rowst[...]
    colrec[me_q] = colst[...]
    for d in pose_peers:
        await_recv(rowrec.at[pabs(*d)], row_recv.at[d[0] * 4 + d[1]])
    for d in text_peers:
        a = qabs(d[0], d[1]) * 2 + (core + d[2]) % 2
        await_recv(colrec.at[a], col_recv.at[(d[0] * 4 + d[1]) * 2 + d[2]])

    def lse_of(parts):
        m = parts[0]
        for p in parts[1:]:
            m = jnp.maximum(m, p)
        s = jnp.exp2(parts[0] - m)
        for p in parts[1:]:
            s = s + jnp.exp2(p - m)
        return m + jnp.log2(s)

    rowall, colall = rowrec.at[8], colrec.at[16]
    rowall[0:8] = lse_of([rowrec[k, 0:8, :] for k in range(8)])
    colall[...] = lse_of([colrec[k] for k in range(16)])
    for i in range(8):
        a = pabs(*ORDER[i])
        rlt[i] = jnp.broadcast_to(rowall[pl.ds(a, 1), :] + 1.0, (U, U)).T
        idt[i] = jnp.broadcast_to(rowrec[a, 8:9, :], (U, U)).T

    macc[...] = jnp.zeros_like(macc)
    lane = lax.broadcasted_iota(jnp.int32, (1, U), 1)
    done = set()

    def slope(i, j):
        if (i, j) in done:
            return
        done.add((i, j))
        rl, ids = rlt[i], idt[i]
        dy, dz = ORDER[j]
        acc = None
        for dc in range(2):
            cols = rows_of(2 * j + dc)
            p = qabs(dy, dz) * 2 + (core + dc) % 2
            base = (p * 8 + (ylo + dy) % 2 * 4 + x) * U
            v = lg[rows_of(i), cols]
            cl = colall[pl.ds(p, 1), :] + 1.0
            hit = ids == (base + lane).astype(F32)
            g = jnp.exp2(v - rl) + jnp.exp2(v - cl)
            t = jnp.where(hit, v, 0.0)
            acc = t if acc is None else acc + t
            hi, lo = split(jnp.where(hit, g - 1.0, g))
            sl[0, rows_of(i), cols] = hi
            sl[1, rows_of(i), cols] = lo
        macc[...] += jnp.sum(acc.reshape(U // 8, 8, U), axis=0)

    def slope_row(i):
        for j in range(8):
            slope(i, j)

    def slope_col(j):
        for i in range(8):
            slope(i, j)

    def pose_unit(i):
        r = rows_of(i)
        sh, sw = sl[0, r, :], sl[1, r, :]
        gp[i] = dot_nn(sh, thl[0]) + dot_nn(sh, thl[1]) + dot_nn(sw, thl[0])

    def text_pair(j):
        c = cols_of(j)
        sh, sw = sl[0, :, c], sl[1, :, c]
        g = dot_nn(xt[0], sh) + dot_nn(xt[0], sw) + dot_nn(xt[1], sh)
        gt[2 * j] = g[:, 0:U]
        gt[2 * j + 1] = g[:, U:]
        copy(gt.at[2 * j + 1], rsib.at[j], rsib_send.at[j], rsib_recv.at[j], text_peer(0, 0, 1))

    def g_at(kind, place):
        return gp.at[SLOT[place]] if kind == 0 else gt.at[2 * SLOT[place]]

    def r_at(kind, i):
        return (rp if kind == 0 else rt).at[i]

    def half(ref, h):
        n = ref.shape[0] // 2
        return ref.at[pl.ds(h * n, n)]

    rs_count = [0, 0]
    def rs_send_to(kind, slot, h, to, i):
        n = rs_count[kind]
        rs_count[kind] += 1
        copy(
            half(g_at(kind, slot), h),
            half(r_at(kind, i), h),
            rs_send.at[kind, n],
            rs_recv.at[kind, i * 2 + h],
            peer(kind, *to),
        )

    def rs_add(kind, slot, i, h):
        await_recv(half(r_at(kind, i), h), rs_recv.at[kind, i * 2 + h])
        dst, src = half(g_at(kind, slot), h), half(r_at(kind, i), h)
        dst[...] += src[...]

    def sib_add(j):
        await_recv(rsib.at[j], rsib_recv.at[j])
        gt[2 * j] += rsib[j]

    def stage_a(kind):
        for h in range(2):
            rs_send_to(kind, (1, 2), h, PAR, 0)

    def stage_b(kind):
        for h in range(2):
            rs_send_to(kind, (1, 1), h, NXT, 1)
            rs_send_to(kind, (1, 3), h, PRV, 2)

    def stage_c(kind):
        rs_add(kind, (0, 2), 0, 0)
        rs_send_to(kind, (0, 2), 0, PRV, 3)
        rs_add(kind, (0, 2), 0, 1)
        rs_send_to(kind, (0, 2), 1, NXT, 3)

    def stage_d(kind):
        for h in range(2):
            rs_add(kind, (1, 0), 1, h)
            rs_add(kind, (1, 0), 2, h)
            rs_send_to(kind, (1, 0), h, PAR, 4)

    def stage_e(kind):
        rs_send_to(kind, (0, 3), 1, PRV, 5)
        rs_send_to(kind, (0, 1), 0, NXT, 6)
        rs_add(kind, (0, 3), 3, 0)
        rs_send_to(kind, (0, 3), 0, PRV, 5)
        rs_add(kind, (0, 1), 3, 1)
        rs_send_to(kind, (0, 1), 1, NXT, 6)

    def loss_first():
        own = 0.5 * (rowall[pl.ds(me_p, 1), :] + colall[pl.ds(me_q, 1), :])
        first = lax.broadcasted_iota(jnp.int32, (8, U), 0) == 0
        la[me_p] = jnp.where(first, jnp.broadcast_to(own, (8, U)), 0.0) - macc[...]
        b = la.at[me_p]
        for n, d in enumerate(pose_peers):
            copy(b, b, la_send.at[n], la_recv.at[(-d[0]) % 2 * 4 + (-d[1]) % 4], pose_peer(*d))

    def loss_second():
        for d in pose_peers:
            await_recv(la.at[pabs(*d)], la_recv.at[d[0] * 4 + d[1]])
        t = la[0]
        for j in range(1, 8):
            t = t + la[j]
        lb[me_q] = t
        b = lb.at[me_q]
        for n, d in enumerate(text_peers):
            copy(
                b,
                b,
                lb_send.at[n],
                lb_recv.at[((-d[0]) % 2 * 4 + (-d[1]) % 4) * 2 + d[2]],
                text_peer(*d),
            )

    slope_row(7)
    slope_col(7)
    pose_unit(7)
    stage_a(0)
    slope_row(6)
    text_pair(7)
    slope_row(5)
    pose_unit(6)
    slope_col(6)
    pose_unit(5)
    stage_b(0)
    sib_add(7)
    stage_a(1)
    slope_col(5)
    text_pair(6)
    slope_row(4)
    text_pair(5)
    slope_col(4)
    pose_unit(4)
    stage_c(0)
    sib_add(6)
    sib_add(5)
    stage_b(1)
    slope_row(3)
    text_pair(4)
    slope_col(3)
    pose_unit(3)
    stage_d(0)
    sib_add(4)
    stage_c(1)
    slope_row(2)
    text_pair(3)
    slope_row(1)
    slope_col(2)
    pose_unit(2)
    slope_row(0)
    pose_unit(1)
    stage_e(0)
    loss_first()
    sib_add(3)
    stage_d(1)
    text_pair(2)
    text_pair(1)
    sib_add(2)
    sib_add(1)
    stage_e(1)
    pose_unit(0)
    text_pair(0)
    loss_second()
    sib_add(0)

    for h in range(2):
        for i in (4, 5, 6):
            rs_add(0, (0, 0), i, h)
    pg_ref[...] = scale * gp[0]
    for d in text_peers:
        a = qabs(d[0], d[1]) * 2 + (core + d[2]) % 2
        await_recv(lb.at[a], lb_recv.at[(d[0] * 4 + d[1]) * 2 + d[2]])
    t = lb[0]
    for j in range(1, 16):
        t = t + lb[j]
    loss_ref[0, 0] = jnp.sum(t) / (total * LOG2E)
    for h in range(2):
        for i in (4, 5, 6):
            rs_add(1, (0, 0), i, h)
    tg_ref[...] = (scale * gt[0]).T

    for c in pending:
        c.wait_send()


def per_device(pose_emb, text_emb, positive):
    rows, width = pose_emb.shape
    total = rows * lax.axis_size("pose") * lax.axis_size("text")
    scale = 2.0 / math.sqrt(width)
    dma = pltpu.SemaphoreType.DMA
    vmem = pltpu.VMEM
    full = pl.BlockSpec(memory_space=pltpu.VMEM)
    loss, pose_grad, text_grad = pl.pallas_call(
        functools.partial(kernel, scale, total),
        out_shape=(
            jax.ShapeDtypeStruct((1, 1), F32),
            jax.ShapeDtypeStruct((rows, width), F32),
            jax.ShapeDtypeStruct((rows, width), F32),
        ),
        in_specs=[full] * 3,
        out_specs=(pl.BlockSpec(memory_space=pltpu.SMEM), full, full),
        scratch_shapes=[
            vmem((8, U, width), F32),
            vmem((16, U, width), F32),
            vmem((2, 8 * U, width), BF16),
            vmem((2, width, 8 * U), BF16),
            vmem((2, 16 * U, width), BF16),
            vmem((8 * U, 16 * U), F32),
            vmem((2, 8 * U, 16 * U), BF16),
            vmem((8, U, width), F32),
            vmem((16, width, U), F32),
            vmem((7, U, width), F32),
            vmem((7, width, U), F32),
            vmem((8, width, U), F32),
            vmem((8, U, U), F32),
            vmem((8, U, U), F32),
            vmem((8, 16 * U), F32),
            vmem((8, 16 * U), F32),
            vmem((8, U, U), F32),
            vmem((8, U, U), F32),
            vmem((16, U), F32),
            vmem((16, U), F32),
            vmem((9, 16, U), F32),
            vmem((17, 16, U), F32),
            vmem((8, 8, U), F32),
            vmem((16, 8, U), F32),
            vmem((8, U), F32),
            dma((2, 16)),
            dma((2, 16)),
            dma((16,)),
            dma((16,)),
            dma((8,)),
            dma((8,)),
            dma((16,)),
            dma((16,)),
            dma((8,)),
            dma((8,)),
            dma((16,)),
            dma((16,)),
            dma((2, 16)),
            dma((2, 16)),
            dma((8,)),
            dma((8,)),
        ],
        compiler_params=pltpu.CompilerParams(
            collective_id=0, has_side_effects=True, vmem_limit_bytes=64 * 1024 * 1024 - 64 * 1024
        ),
    )(pose_emb, text_emb, positive.reshape(1, rows))
    return (loss.reshape(()), pose_grad, text_grad)


def solution(mesh):
    return jax.shard_map(
        per_device,
        mesh=mesh,
        in_specs=(P(("pose", "text"), None), P(("pose", "text"), None), P(("pose", "text"))),
        out_specs=(P(), P(("pose", "text"), None), P(("pose", "text"), None)),
        check_vma=False,
    )
```

```python
import functools
import math

import jax
import jax.numpy as jnp
from jax import lax
from jax.experimental import pallas as pl
from jax.experimental.pallas import tpu as pltpu
from jax.sharding import PartitionSpec as P

F32 = jnp.float32
BF16 = jnp.bfloat16
U = 128
H = U // 2
LOG2E = math.log2(math.e)


def split(v):
    hi = v.astype(BF16)
    return hi, (v - hi.astype(F32)).astype(BF16)


def dot_nn(a, b):
    return jnp.dot(a, b, preferred_element_type=F32)


ORDER = [(0, 0), (0, 3), (0, 1), (1, 0), (0, 2), (1, 3), (1, 1), (1, 2)]
SLOT = {place: k for k, place in enumerate(ORDER)}
NXT, PRV, PAR = (0, 1), (0, 3), (1, 0)


def kernel(
    scale,
    total,
    pose_ref,
    text_ref,
    pos_ref,
    loss_ref,
    pg_ref,
    tg_ref,
    xf,
    tf,
    xhl,
    xt,
    thl,
    lg,
    sl,
    gp,
    gt,
    rp,
    rt,
    rsib,
    rm,
    rs,
    cm,
    cs,
    rlt,
    idt,
    rowst,
    colst,
    rowrec,
    colrec,
    la,
    lb,
    macc,
    ag_send,
    ag_recv,
    sib_send,
    sib_recv,
    row_send,
    row_recv,
    col_send,
    col_recv,
    la_send,
    la_recv,
    lb_send,
    lb_recv,
    rs_send,
    rs_recv,
    rsib_send,
    rsib_recv,
):
    width = pose_ref.shape[1]
    pi = lax.axis_index("pose")
    ti = lax.axis_index("text")
    yhi, z, core = pi // 8, (pi // 2) % 4, pi % 2
    ylo, x = ti // 4, ti % 4

    def pabs(dy, dx):
        return (ylo + dy) % 2 * 4 + (x + dx) % 4

    def qabs(dy, dz):
        return (yhi + dy) % 2 * 4 + (z + dz) % 4

    def pose_peer(dy, dx):
        return (pi, pabs(dy, dx))

    def text_peer(dy, dz, dc=0):
        return (qabs(dy, dz) * 2 + (core + dc) % 2, (ylo + dy) % 2 * 4 + x)

    pose_peers = [(dy, dx) for dy in range(2) for dx in range(4) if (dy, dx) != (0, 0)]
    text_peers = [
        (dy, dz, dc)
        for dy in range(2)
        for dz in range(4)
        for dc in range(2)
        if (dy, dz, dc) != (0, 0, 0)
    ]

    barrier = pltpu.get_barrier_semaphore()
    near_by = [pose_peer(*d) for d in (NXT, PRV, PAR)]
    near_by += [text_peer(*d) for d in (NXT, PRV, PAR)] + [text_peer(0, 0, 1)]
    for d in near_by:
        pl.semaphore_signal(barrier, inc=1, device_id=d, device_id_type=pl.DeviceIdType.MESH)
    me_p = pabs(0, 0)
    me_q = pi
    xf[me_p] = pose_ref[...]
    tf[me_q] = text_ref[...]
    pl.semaphore_wait(barrier, len(near_by))

    pending = []

    def copy(src, dst, ssem, rsem, dev):
        c = pltpu.make_async_remote_copy(
            src_ref=src,
            dst_ref=dst,
            send_sem=ssem,
            recv_sem=rsem,
            device_id=dev,
            device_id_type=pl.DeviceIdType.MESH,
        )
        c.start()
        pending.append(c)
        return c

    def await_recv(dst, rsem):
        pltpu.make_async_copy(dst, dst, rsem).wait()

    def buf(kind, dy, dd, h):
        if kind == 0:
            return xf.at[pabs(dy, dd), pl.ds(h * H, H)]
        return tf.at[qabs(dy, dd) * 2 + core, pl.ds(h * H, H)]

    def sib_buf(dy, dd, h, mine):
        c = core if mine else 1 - core
        return tf.at[qabs(dy, dd) * 2 + c, pl.ds(h * H, H)]

    def peer(kind, dy, dd):
        return pose_peer(dy, dd) if kind == 0 else text_peer(dy, dd, 0)

    send_count = [0, 0]

    def send(kind, src, h, to, arrives):
        n = send_count[kind]
        send_count[kind] += 1
        b = buf(kind, *src, h)
        copy(b, b, ag_send.at[kind, n], ag_recv.at[kind, SLOT[arrives] * 2 + h], peer(kind, *to))

    def got(kind, place, h):
        await_recv(buf(kind, *place, h), ag_recv.at[kind, SLOT[place] * 2 + h])
        if kind == 1:
            share(place, h)

    def share(place, h):
        i = SLOT[place] * 2 + h
        b = sib_buf(*place, h, True)
        copy(b, b, sib_send.at[i], sib_recv.at[i], text_peer(0, 0, 1))

    def got_sib(place):
        for h in range(2):
            i = SLOT[place] * 2 + h
            await_recv(sib_buf(*place, h, False), sib_recv.at[i])

    def rows_of(i, n=1):
        return slice(i * U, (i + n) * U)

    def cols_of(j, n=1):
        return slice(j * 2 * U, (j + n) * 2 * U)

    def convert_pose(i):
        v = xf[pabs(*ORDER[i])]
        xhl[0, rows_of(i), :], xhl[1, rows_of(i), :] = split(v)
        xt[0, :, rows_of(i)], xt[1, :, rows_of(i)] = split(v.T)

    def convert_text(j, dc):
        v = tf[qabs(*ORDER[j]) * 2 + (core + dc) % 2]
        rows = rows_of(2 * j + dc)
        thl[0, rows, :], thl[1, rows, :] = split(v)
        sl[0, 0:width, rows], sl[1, 0:width, rows] = split(v.T)

    seen_row, seen_col = set(), set()

    def stats(i, j):
        v = lg[rows_of(i), cols_of(j)]
        a, b = v[:, 0:U], v[:, U:]
        top = jnp.maximum(a, b)
        if i in seen_row:
            old = rm[i]
            top = jnp.maximum(top, old)
            rs[i] = rs[i] * jnp.exp2(old - top) + jnp.exp2(a - top) + jnp.exp2(b - top)
        else:
            rs[i] = jnp.exp2(a - top) + jnp.exp2(b - top)
        rm[i] = top
        w = v.reshape(U // 8, 8, 2 * U)
        top = jnp.max(w, axis=0)
        if j in seen_col:
            old = cm[:, cols_of(j)]
            top = jnp.maximum(top, old)
            cs[:, cols_of(j)] = cs[:, cols_of(j)] * jnp.exp2(old - top) + jnp.sum(jnp.exp2(w - top[None]), axis=0)
        else:
            cs[:, cols_of(j)] = jnp.sum(jnp.exp2(w - top[None]), axis=0)
        cm[:, cols_of(j)] = top
        seen_row.add(i)
        seen_col.add(j)

    waiting = []

    def logits(i, n, j):
        r, c = rows_of(i, n), cols_of(j)
        xh, xl = xhl[0, r, :], xhl[1, r, :]
        th, tl = sl[0, 0:width, c], sl[1, 0:width, c]
        value = (scale * LOG2E) * (dot_nn(xh, th) + dot_nn(xl, th) + dot_nn(xh, tl))
        flush()
        lg[r, c] = value
        waiting.extend((k, j) for k in range(i, i + n))

    def flush():
        for k, j in waiting:
            stats(k, j)
        waiting.clear()

    for h in range(2):
        for kind in range(2):
            send(kind, (0, 0), h, NXT, (0, 3))
            send(kind, (0, 0), 1 - h, PRV, (0, 1))
            send(kind, (0, 0), h, PAR, (1, 0))
        share((0, 0), h)
    convert_pose(0)
    convert_text(0, 0)

    for kind in range(2):
        got(kind, (0, 3), 0)
        send(kind, (0, 3), 0, NXT, (0, 2))
        got(kind, (0, 1), 1)
        send(kind, (0, 1), 1, PRV, (0, 2))
    for kind in range(2):
        got(kind, (1, 0), 0)
        send(kind, (1, 0), 0, NXT, (1, 3))
        send(kind, (1, 0), 0, PRV, (1, 1))
    got_sib((0, 0))
    convert_text(0, 1)
    for kind in range(2):
        got(kind, (0, 3), 1)
        got(kind, (0, 1), 0)
    for kind in range(2):
        got(kind, (1, 0), 1)
        send(kind, (1, 0), 1, NXT, (1, 3))
        send(kind, (1, 0), 1, PRV, (1, 1))
    for i in (1, 2, 3):
        convert_pose(i)
        convert_text(i, 0)
    for j in (1, 2, 3):
        got_sib(ORDER[j])
        convert_text(j, 1)
    for j in range(4):
        logits(0, 4, j)
    for h in range(2):
        for kind in range(2):
            got(kind, (0, 2), h)
            send(kind, (0, 2), h, PAR, (1, 2))
    convert_pose(4)
    convert_text(4, 0)
    got_sib((0, 2))
    convert_text(4, 1)
    for j in range(4):
        logits(4, 1, j)
    logits(0, 5, 4)
    flush()
    for i in (5, 6):
        for h in range(2):
            got(0, ORDER[i], h)
        convert_pose(i)
    for i in (5, 6):
        for h in range(2):
            got(1, ORDER[i], h)
        convert_text(i, 0)
    for j in range(5):
        logits(5, 2, j)
    for j in (5, 6):
        got_sib(ORDER[j])
        convert_text(j, 1)
        logits(0, 7, j)
    for kind in range(2):
        for h in range(2):
            got(kind, (1, 2), h)
    convert_pose(7)
    convert_text(7, 0)
    for j in range(7):
        logits(7, 1, j)
    got_sib((1, 2))
    convert_text(7, 1)
    logits(0, 8, 7)
    flush()

    for i in range(8):
        mt, st = rm[i].T, rs[i].T
        m = jnp.max(mt, axis=0, keepdims=True)
        s = jnp.sum(st * jnp.exp2(mt - m), axis=0, keepdims=True)
        rowst[pl.ds(pabs(*ORDER[i]), 1), :] = m + jnp.log2(s)
    rowst[8:16, :] = jnp.broadcast_to(pos_ref[...].astype(F32), (8, U))
    m = jnp.max(cm[...], axis=0, keepdims=True)
    s = jnp.sum(cs[...] * jnp.exp2(cm[...] - m), axis=0, keepdims=True)
    lse = m + jnp.log2(s)
    for j in range(8):
        for dc in range(2):
            p = qabs(*ORDER[j]) * 2 + (core + dc) % 2
            colst[pl.ds(p, 1), :] = lse[:, rows_of(2 * j + dc)]

    for n, d in enumerate(pose_peers):
        copy(rowst, rowrec.at[me_p], row_send.at[n], row_recv.at[(-d[0]) % 2 * 4 + (-d[1]) % 4], pose_peer(*d))
    for n, d in enumerate(text_peers):
        copy(
            colst,
            colrec.at[me_q],
            col_send.at[n],
            col_recv.at[((-d[0]) % 2 * 4 + (-d[1]) % 4) * 2 + d[2]],
            text_peer(*d),
        )
    rowrec[me_p] = rowst[...]
    colrec[me_q] = colst[...]
    for d in pose_peers:
        await_recv(rowrec.at[pabs(*d)], row_recv.at[d[0] * 4 + d[1]])
    for d in text_peers:
        a = qabs(d[0], d[1]) * 2 + (core + d[2]) % 2
        await_recv(colrec.at[a], col_recv.at[(d[0] * 4 + d[1]) * 2 + d[2]])

    def lse_of(parts):
        m = parts[0]
        for p in parts[1:]:
            m = jnp.maximum(m, p)
        s = jnp.exp2(parts[0] - m)
        for p in parts[1:]:
            s = s + jnp.exp2(p - m)
        return m + jnp.log2(s)

    rowall, colall = rowrec.at[8], colrec.at[16]
    rowall[0:8] = lse_of([rowrec[k, 0:8, :] for k in range(8)])
    colall[...] = lse_of([colrec[k] for k in range(16)])
    for i in range(8):
        a = pabs(*ORDER[i])
        rlt[i] = jnp.broadcast_to(rowall[pl.ds(a, 1), :] + 1.0, (U, U)).T
        idt[i] = jnp.broadcast_to(rowrec[a, 8:9, :], (U, U)).T

    macc[...] = jnp.zeros_like(macc)
    lane = lax.broadcasted_iota(jnp.int32, (1, U), 1)
    done = set()

    def slope(i, j):
        if (i, j) in done:
            return
        done.add((i, j))
        rl, ids = rlt[i], idt[i]
        dy, dz = ORDER[j]
        acc = None
        for dc in range(2):
            cols = rows_of(2 * j + dc)
            p = qabs(dy, dz) * 2 + (core + dc) % 2
            base = (p * 8 + (ylo + dy) % 2 * 4 + x) * U
            v = lg[rows_of(i), cols]
            cl = colall[pl.ds(p, 1), :] + 1.0
            hit = ids == (base + lane).astype(F32)
            g = jnp.exp2(v - rl) + jnp.exp2(v - cl)
            t = jnp.where(hit, v, 0.0)
            acc = t if acc is None else acc + t
            hi, lo = split(jnp.where(hit, g - 1.0, g))
            sl[0, rows_of(i), cols] = hi
            sl[1, rows_of(i), cols] = lo
        macc[...] += jnp.sum(acc.reshape(U // 8, 8, U), axis=0)

    def slope_row(i):
        for j in range(8):
            slope(i, j)

    def slope_col(j):
        for i in range(8):
            slope(i, j)

    def pose_unit(i):
        r = rows_of(i)
        sh, sw = sl[0, r, :], sl[1, r, :]
        gp[i] = dot_nn(sh, thl[0]) + dot_nn(sh, thl[1]) + dot_nn(sw, thl[0])

    def text_pair(j):
        c = cols_of(j)
        sh, sw = sl[0, :, c], sl[1, :, c]
        g = dot_nn(xt[0], sh) + dot_nn(xt[0], sw) + dot_nn(xt[1], sh)
        gt[2 * j] = g[:, 0:U]
        gt[2 * j + 1] = g[:, U:]
        copy(gt.at[2 * j + 1], rsib.at[j], rsib_send.at[j], rsib_recv.at[j], text_peer(0, 0, 1))

    def g_at(kind, place):
        return gp.at[SLOT[place]] if kind == 0 else gt.at[2 * SLOT[place]]

    def r_at(kind, i):
        return (rp if kind == 0 else rt).at[i]

    def half(ref, h):
        n = ref.shape[0] // 2
        return ref.at[pl.ds(h * n, n)]

    rs_count = [0, 0]
    def rs_send_to(kind, slot, h, to, i):
        n = rs_count[kind]
        rs_count[kind] += 1
        copy(
            half(g_at(kind, slot), h),
            half(r_at(kind, i), h),
            rs_send.at[kind, n],
            rs_recv.at[kind, i * 2 + h],
            peer(kind, *to),
        )

    def rs_add(kind, slot, i, h):
        await_recv(half(r_at(kind, i), h), rs_recv.at[kind, i * 2 + h])
        dst, src = half(g_at(kind, slot), h), half(r_at(kind, i), h)
        dst[...] += src[...]

    def sib_add(j):
        await_recv(rsib.at[j], rsib_recv.at[j])
        gt[2 * j] += rsib[j]

    def pass_on(step, kind, h):
        if step == "a":
            rs_send_to(kind, (1, 2), h, PAR, 0)
        elif step == "b1":
            rs_send_to(kind, (1, 1), h, NXT, 1)
        elif step == "b2":
            rs_send_to(kind, (1, 3), h, PRV, 2)
        elif step == "c":
            rs_add(kind, (0, 2), 0, h)
            rs_send_to(kind, (0, 2), h, (PRV, NXT)[h], 3)
        elif step == "d":
            rs_add(kind, (1, 0), 1, h)
            rs_add(kind, (1, 0), 2, h)
            rs_send_to(kind, (1, 0), h, PAR, 4)
        else:
            place = (0, 3) if step in ("e0", "f0") else (0, 1)
            if step in ("f0", "f1"):
                rs_add(kind, place, 3, h)
            rs_send_to(kind, place, h, PRV if place == (0, 3) else NXT, 5 if place == (0, 3) else 6)

    def loss_first():
        own = 0.5 * (rowall[pl.ds(me_p, 1), :] + colall[pl.ds(me_q, 1), :])
        first = lax.broadcasted_iota(jnp.int32, (8, U), 0) == 0
        la[me_p] = jnp.where(first, jnp.broadcast_to(own, (8, U)), 0.0) - macc[...]
        b = la.at[me_p]
        for n, d in enumerate(pose_peers):
            copy(b, b, la_send.at[n], la_recv.at[(-d[0]) % 2 * 4 + (-d[1]) % 4], pose_peer(*d))

    def loss_second():
        for d in pose_peers:
            await_recv(la.at[pabs(*d)], la_recv.at[d[0] * 4 + d[1]])
        t = la[0]
        for j in range(1, 8):
            t = t + la[j]
        lb[me_q] = t
        b = lb.at[me_q]
        for n, d in enumerate(text_peers):
            copy(
                b,
                b,
                lb_send.at[n],
                lb_recv.at[((-d[0]) % 2 * 4 + (-d[1]) % 4) * 2 + d[2]],
                text_peer(*d),
            )

    plan = [
        ("T", 7, 0), ("P", 6, 0), ("b1", 0, 0), ("b1", 0, 1), ("P", 7, 0), ("a", 0, 0),
        ("a", 0, 1), ("W", 7, 0), ("a", 1, 0), ("a", 1, 1), ("T", 5, 0), ("T", 6, 0),
        ("P", 5, 0), ("b2", 0, 0), ("b2", 0, 1), ("P", 4, 0), ("W", 5, 0), ("b2", 1, 0),
        ("b2", 1, 1), ("W", 6, 0), ("b1", 1, 0), ("b1", 1, 1), ("c", 0, 0), ("T", 4, 0),
        ("T", 3, 0), ("c", 0, 1), ("T", 2, 0), ("T", 1, 0), ("W", 4, 0), ("c", 1, 0),
        ("c", 1, 1), ("W", 3, 0), ("d", 1, 0), ("P", 1, 0), ("e0", 0, 1), ("W", 2, 0),
        ("e1", 1, 0), ("P", 2, 0), ("e1", 0, 0), ("W", 1, 0), ("e0", 1, 1), ("P", 3, 0),
        ("d", 0, 0), ("d", 0, 1), ("d", 1, 1), ("f1", 0, 1), ("f0", 0, 0), ("L1", 0, 0),
        ("P", 0, 0), ("T", 0, 0), ("f0", 1, 0), ("f1", 1, 1), ("W", 0, 0), ("L2", 0, 0),
    ]
    products = [step[:2] for step in plan if step[0] in ("P", "T")]

    def slope_for(step):
        if step[0] == "P":
            slope_row(step[1])
        else:
            slope_col(step[1])

    slope_for(products[0])
    at = 0
    for step, n, h in plan:
        if step in ("P", "T"):
            at += 1
            if at < len(products):
                slope_for(products[at])
            if step == "P":
                pose_unit(n)
            else:
                text_pair(n)
        elif step == "W":
            sib_add(n)
        elif step == "L1":
            loss_first()
        elif step == "L2":
            loss_second()
        else:
            pass_on(step, n, h)

    for h in range(2):
        for i in (4, 5, 6):
            rs_add(0, (0, 0), i, h)
    pg_ref[...] = scale * gp[0]
    for d in text_peers:
        a = qabs(d[0], d[1]) * 2 + (core + d[2]) % 2
        await_recv(lb.at[a], lb_recv.at[(d[0] * 4 + d[1]) * 2 + d[2]])
    t = lb[0]
    for j in range(1, 16):
        t = t + lb[j]
    loss_ref[0, 0] = jnp.sum(t) / (total * LOG2E)
    for h in range(2):
        for i in (4, 5, 6):
            rs_add(1, (0, 0), i, h)
    tg_ref[...] = (scale * gt[0]).T

    for c in pending:
        c.wait_send()


def per_device(pose_emb, text_emb, positive):
    rows, width = pose_emb.shape
    total = rows * lax.axis_size("pose") * lax.axis_size("text")
    scale = 2.0 / math.sqrt(width)
    dma = pltpu.SemaphoreType.DMA
    vmem = pltpu.VMEM
    full = pl.BlockSpec(memory_space=pltpu.VMEM)
    loss, pose_grad, text_grad = pl.pallas_call(
        functools.partial(kernel, scale, total),
        out_shape=(
            jax.ShapeDtypeStruct((1, 1), F32),
            jax.ShapeDtypeStruct((rows, width), F32),
            jax.ShapeDtypeStruct((rows, width), F32),
        ),
        in_specs=[full] * 3,
        out_specs=(pl.BlockSpec(memory_space=pltpu.SMEM), full, full),
        scratch_shapes=[
            vmem((8, U, width), F32),
            vmem((16, U, width), F32),
            vmem((2, 8 * U, width), BF16),
            vmem((2, width, 8 * U), BF16),
            vmem((2, 16 * U, width), BF16),
            vmem((8 * U, 16 * U), F32),
            vmem((2, 8 * U, 16 * U), BF16),
            vmem((8, U, width), F32),
            vmem((16, width, U), F32),
            vmem((7, U, width), F32),
            vmem((7, width, U), F32),
            vmem((8, width, U), F32),
            vmem((8, U, U), F32),
            vmem((8, U, U), F32),
            vmem((8, 16 * U), F32),
            vmem((8, 16 * U), F32),
            vmem((8, U, U), F32),
            vmem((8, U, U), F32),
            vmem((16, U), F32),
            vmem((16, U), F32),
            vmem((9, 16, U), F32),
            vmem((17, 16, U), F32),
            vmem((8, 8, U), F32),
            vmem((16, 8, U), F32),
            vmem((8, U), F32),
            dma((2, 16)),
            dma((2, 16)),
            dma((16,)),
            dma((16,)),
            dma((8,)),
            dma((8,)),
            dma((16,)),
            dma((16,)),
            dma((8,)),
            dma((8,)),
            dma((16,)),
            dma((16,)),
            dma((2, 16)),
            dma((2, 16)),
            dma((8,)),
            dma((8,)),
        ],
        compiler_params=pltpu.CompilerParams(
            collective_id=0, has_side_effects=True, vmem_limit_bytes=64 * 1024 * 1024 - 64 * 1024
        ),
    )(pose_emb, text_emb, positive.reshape(1, rows))
    return (loss.reshape(()), pose_grad, text_grad)


def solution(mesh):
    return jax.shard_map(
        per_device,
        mesh=mesh,
        in_specs=(P(("pose", "text"), None), P(("pose", "text"), None), P(("pose", "text"))),
        out_specs=(P(), P(("pose", "text"), None), P(("pose", "text"), None)),
        check_vma=False,
    )
```

```python
import functools
import math

import jax
import jax.numpy as jnp
from jax import lax
from jax.experimental import pallas as pl
from jax.experimental.pallas import tpu as pltpu
from jax.sharding import PartitionSpec as P

F32 = jnp.float32
BF16 = jnp.bfloat16
U = 128
H = U // 2
LOG2E = math.log2(math.e)


def split(v):
    hi = v.astype(BF16)
    return hi, (v - hi.astype(F32)).astype(BF16)


def dot_nn(a, b):
    return jnp.dot(a, b, preferred_element_type=F32)


ORDER = [(0, 0), (1, 0), (0, 3), (0, 1), (0, 2), (1, 3), (1, 1), (1, 2)]
SLOT = {place: k for k, place in enumerate(ORDER)}
NXT, PRV, PAR = (0, 1), (0, 3), (1, 0)


def kernel(
    scale,
    total,
    pose_ref,
    text_ref,
    pos_ref,
    loss_ref,
    pg_ref,
    tg_ref,
    xf,
    tf,
    xhl,
    xt,
    thl,
    lg,
    sl,
    gp,
    gt,
    rp,
    rt,
    rsib,
    rm,
    rs,
    cm,
    cs,
    rlt,
    idt,
    cv,
    rowst,
    colst,
    rowrec,
    colrec,
    la,
    lb,
    macc,
    ag_send,
    ag_recv,
    sib_send,
    sib_recv,
    group,
    rs_send,
    rs_recv,
    rsib_send,
    rsib_recv,
):
    width = pose_ref.shape[1]
    pi = lax.axis_index("pose")
    ti = lax.axis_index("text")
    yhi, z, core = pi // 8, (pi // 2) % 4, pi % 2
    ylo, x = ti // 4, ti % 4

    def pabs(dy, dx):
        return (ylo + dy) % 2 * 4 + (x + dx) % 4

    def qabs(dy, dz):
        return (yhi + dy) % 2 * 4 + (z + dz) % 4

    def pose_peer(dy, dx):
        return (pi, pabs(dy, dx))

    def text_peer(dy, dz, dc=0):
        return (qabs(dy, dz) * 2 + (core + dc) % 2, (ylo + dy) % 2 * 4 + x)

    pose_peers = [(dy, dx) for dy in range(2) for dx in range(4) if (dy, dx) != (0, 0)]
    text_peers = [
        (dy, dz, dc)
        for dy in range(2)
        for dz in range(4)
        for dc in range(2)
        if (dy, dz, dc) != (0, 0, 0)
    ]

    barrier = pltpu.get_barrier_semaphore()
    near_by = [pose_peer(*d) for d in (NXT, PRV, PAR)]
    near_by += [text_peer(*d) for d in (NXT, PRV, PAR)] + [text_peer(0, 0, 1)]
    for d in near_by:
        pl.semaphore_signal(barrier, inc=1, device_id=d, device_id_type=pl.DeviceIdType.MESH)
    me_p = pabs(0, 0)
    me_q = pi
    xf[me_p] = pose_ref[...]
    tf[me_q] = text_ref[...]
    pl.semaphore_wait(barrier, len(near_by))

    def copy(src, dst, ssem, rsem, dev):
        c = pltpu.make_async_remote_copy(
            src_ref=src,
            dst_ref=dst,
            send_sem=ssem,
            recv_sem=rsem,
            device_id=dev,
            device_id_type=pl.DeviceIdType.MESH,
        )
        c.start()

    def await_recv(dst, rsem):
        pltpu.make_async_copy(dst, dst, rsem).wait()

    def buf(kind, dy, dd, h):
        if kind == 0:
            return xf.at[pabs(dy, dd), pl.ds(h * H, H)]
        return tf.at[qabs(dy, dd) * 2 + core, pl.ds(h * H, H)]

    def peer(kind, dy, dd):
        return pose_peer(dy, dd) if kind == 0 else text_peer(dy, dd, 0)

    def recv_index(place, h):
        return SLOT[place] * 2 + (h if SLOT[place] < 5 else 0)

    def send(kind, src, h, to, arrives):
        b = buf(kind, *src, h)
        copy(b, b, ag_send.at[kind], ag_recv.at[kind, recv_index(arrives, h)], peer(kind, *to))

    def got(kind, place, h):
        await_recv(buf(kind, *place, h), ag_recv.at[kind, SLOT[place] * 2 + h])

    def whole(kind, dy, dd):
        return xf.at[pabs(dy, dd)] if kind == 0 else tf.at[qabs(dy, dd) * 2 + core]

    def got_whole(kind, place):
        await_recv(whole(kind, *place), ag_recv.at[kind, SLOT[place] * 2])

    def share(place):
        b = whole(1, *place)
        copy(b, b, sib_send.at[0], sib_recv.at[SLOT[place]], text_peer(0, 0, 1))

    def got_sib(place):
        await_recv(tf.at[qabs(*place) * 2 + 1 - core], sib_recv.at[SLOT[place]])

    def rows_of(i, n=1):
        return slice(i * U, (i + n) * U)

    def cols_of(j, n=1):
        return slice(j * 2 * U, (j + n) * 2 * U)

    def convert_pose(i):
        v = xf[pabs(*ORDER[i])]
        xhl[0, rows_of(i), :], xhl[1, rows_of(i), :] = split(v)
        xt[0, :, rows_of(i)], xt[1, :, rows_of(i)] = split(v.T)

    def convert_text(j, dc):
        v = tf[qabs(*ORDER[j]) * 2 + (core + dc) % 2]
        rows = rows_of(2 * j + dc)
        thl[0, rows, :], thl[1, rows, :] = split(v)
        sl[0, 0:width, rows], sl[1, 0:width, rows] = split(v.T)

    def stats(i, v, top, total):
        a, b = v[:, 0:U], v[:, U:]
        old = rm[i]
        new = jnp.maximum(jnp.maximum(a, b), old)
        rs[i] = rs[i] * jnp.exp2(old - new) + jnp.exp2(a - new) + jnp.exp2(b - new)
        rm[i] = new
        w = v.reshape(U // 8, 8, 2 * U)
        new = jnp.maximum(top, jnp.max(w, axis=0))
        return new, total * jnp.exp2(top - new) + jnp.sum(jnp.exp2(w - new[None]), axis=0)

    def logits(i, n, j, count=1):
        def body(jj):
            c = pl.ds(pl.multiple_of(jj * 2 * U, 2 * U), 2 * U)
            th, tl = sl[0, 0:width, c], sl[1, 0:width, c]
            top, total = cm[:, c], cs[:, c]
            k = i
            while k < i + n:
                m = min(2, i + n - k)
                r = rows_of(k, m)
                xh, xl = xhl[0, r, :], xhl[1, r, :]
                v = (scale * LOG2E) * (dot_nn(xh, th) + dot_nn(xl, th) + dot_nn(xh, tl))
                lg[r, c] = v
                for q in range(m):
                    top, total = stats(k + q, v[rows_of(q)], top, total)
                k += m
            cm[:, c], cs[:, c] = top, total

        if count == 1:
            body(j)
        else:

            def step(jj, carry):
                body(jj)
                return carry

            lax.fori_loop(j, j + count, step, 0)

    for ref in (rm, cm):
        ref[...] = jnp.full_like(ref, -jnp.inf)
    for ref in (rs, cs):
        ref[...] = jnp.zeros_like(ref)

    for h in range(2):
        for kind in range(2):
            send(kind, (0, 0), h, NXT, (0, 3))
            send(kind, (0, 0), 1 - h, PRV, (0, 1))
            send(kind, (0, 0), h, PAR, (1, 0))
    share((0, 0))
    convert_pose(0)
    convert_text(0, 0)

    for kind in range(2):
        got(kind, (0, 3), 0)
        send(kind, (0, 3), 0, NXT, (0, 2))
        got(kind, (0, 1), 1)
        send(kind, (0, 1), 1, PRV, (0, 2))
    for kind in range(2):
        got(kind, (1, 0), 0)
        send(kind, (1, 0), 0, NXT, (1, 3))
        send(kind, (1, 0), 0, PRV, (1, 1))
    got_sib((0, 0))
    convert_text(0, 1)
    for kind in range(2):
        got(kind, (0, 3), 1)
        got(kind, (0, 1), 0)
    for kind in range(2):
        got(kind, (1, 0), 1)
        send(kind, (1, 0), 1, NXT, (1, 3))
        send(kind, (1, 0), 1, PRV, (1, 1))
    for i in (1, 2, 3):
        share(ORDER[i])
    for i in (1, 2, 3):
        convert_pose(i)
        convert_text(i, 0)
    for j in (1, 2, 3):
        got_sib(ORDER[j])
        convert_text(j, 1)
    logits(0, 4, 0, 4)
    for h in range(2):
        for kind in range(2):
            got(kind, (0, 2), h)
            send(kind, (0, 2), h, PAR, (1, 2))
    share((0, 2))
    convert_pose(4)
    convert_text(4, 0)
    got_sib((0, 2))
    convert_text(4, 1)
    logits(4, 1, 0, 4)
    logits(0, 5, 4)
    for i in (5, 6):
        got_whole(0, ORDER[i])
        convert_pose(i)
    for i in (5, 6):
        got_whole(1, ORDER[i])
        share(ORDER[i])
        convert_text(i, 0)
    logits(5, 2, 0, 5)
    for j in (5, 6):
        got_sib(ORDER[j])
        convert_text(j, 1)
    logits(0, 7, 5, 2)
    for kind in range(2):
        got_whole(kind, (1, 2))
    share((1, 2))
    convert_pose(7)
    convert_text(7, 0)
    logits(7, 1, 0, 7)
    got_sib((1, 2))
    convert_text(7, 1)
    logits(0, 8, 7)

    for i in range(8):
        mt, st = rm[i].T, rs[i].T
        m = jnp.max(mt, axis=0, keepdims=True)
        s = jnp.sum(st * jnp.exp2(mt - m), axis=0, keepdims=True)
        rowst[pl.ds(pabs(*ORDER[i]), 1), :] = m + jnp.log2(s)
    rowst[8:16, :] = jnp.broadcast_to(pos_ref[...].astype(F32), (8, U))
    m = jnp.max(cm[...], axis=0, keepdims=True)
    s = jnp.sum(cs[...] * jnp.exp2(cm[...] - m), axis=0, keepdims=True)
    lse = m + jnp.log2(s)
    for j in range(8):
        for dc in range(2):
            p = qabs(*ORDER[j]) * 2 + (core + dc) % 2
            colst[pl.ds(p, 1), :] = lse[:, rows_of(2 * j + dc)]

    for d in pose_peers:
        copy(rowst, rowrec.at[me_p], group.at[0], group.at[1], pose_peer(*d))
    for d in text_peers:
        copy(colst, colrec.at[me_q], group.at[2], group.at[3], text_peer(*d))
    rowrec[me_p] = rowst[...]
    colrec[me_q] = colst[...]
    await_recv(rowrec.at[0:7], group.at[1])
    await_recv(colrec.at[0:15], group.at[3])

    def lse_of(parts):
        m = parts[0]
        for p in parts[1:]:
            m = jnp.maximum(m, p)
        s = jnp.exp2(parts[0] - m)
        for p in parts[1:]:
            s = s + jnp.exp2(p - m)
        return m + jnp.log2(s)

    rowall, colall = rowrec.at[8], colrec.at[16]
    rowall[0:8] = lse_of([rowrec[k, 0:8, :] for k in range(8)])
    colall[...] = lse_of([colrec[k] for k in range(16)])
    for i in range(8):
        a = pabs(*ORDER[i])
        rlt[i] = jnp.broadcast_to(rowall[pl.ds(a, 1), :] + 1.0, (U, U)).T
        idt[i] = jnp.broadcast_to(rowrec[a, 8:9, :], (U, U)).T

    macc[...] = jnp.zeros_like(macc)
    lane = lax.broadcasted_iota(jnp.int32, (1, U), 1)
    for j, (dy, dz) in enumerate(ORDER):
        for dc in range(2):
            p = qabs(dy, dz) * 2 + (core + dc) % 2
            base = (p * 8 + (ylo + dy) % 2 * 4 + x) * U
            cv[0:1, rows_of(2 * j + dc)] = colall[pl.ds(p, 1), :] + 1.0
            cv[1:2, rows_of(2 * j + dc)] = (base + lane).astype(F32)

    def loop(lo, hi, body):
        def step(k, carry):
            body(k)
            return carry

        if hi > lo:
            lax.fori_loop(lo, hi, step, 0)

    def slope(i2, j):
        acc = None
        for u in range(2):
            rl, ids = rlt[2 * i2 + u], idt[2 * i2 + u]
            r = pl.ds(pl.multiple_of((2 * i2 + u) * U, U), U)
            for dc in range(2):
                c = pl.ds(pl.multiple_of((2 * j + dc) * U, U), U)
                v = lg[r, c]
                hit = ids == cv[1:2, c]
                g = jnp.exp2(v - rl) + jnp.exp2(v - cv[0:1, c])
                t = jnp.where(hit, v, 0.0)
                acc = t if acc is None else acc + t
                hi, lo = split(jnp.where(hit, g - 1.0, g))
                sl[0, r, c] = hi
                sl[1, r, c] = lo
        macc[...] += jnp.sum(acc.reshape(U // 8, 8, U), axis=0)

    reach = {"wide": 8, "tall": 8}

    def slope_for(step, n):
        if step == "Q":
            loop(0, reach["wide"], lambda j: slope(n // 2, j))
            reach["tall"] = n
        else:
            new = min(n, reach["wide"])
            if new < reach["wide"]:
                for j in range(new, reach["wide"]):
                    loop(0, reach["tall"] // 2, lambda i2, j=j: slope(i2, j))
                reach["wide"] = new

    def pose_pair(i):
        r = rows_of(i, 2)

        def body(k):
            c = pl.ds(pl.multiple_of(k * 2 * U, 2 * U), 2 * U)
            sh, sw = sl[0, r, :], sl[1, r, :]
            th = thl[0, :, c]
            g = dot_nn(sh, th) + dot_nn(sh, thl[1, :, c]) + dot_nn(sw, th)
            gp[i, :, c] = g[0:U]
            gp[i + 1, :, c] = g[U:]

        loop(0, width // (2 * U), body)

    def text_pair(j):
        c = cols_of(j)

        def body(k):
            r = pl.ds(pl.multiple_of(k * 2 * U, 2 * U), 2 * U)
            sh, sw = sl[0, :, c], sl[1, :, c]
            xh = xt[0, r, :]
            g = dot_nn(xh, sh) + dot_nn(xh, sw) + dot_nn(xt[1, r, :], sh)
            gt[2 * j, r, :] = g[:, 0:U]
            gt[2 * j + 1, r, :] = g[:, U:]

        loop(0, width // (2 * U), body)
        copy(gt.at[2 * j + 1], rsib.at[j], rsib_send.at[0], rsib_recv.at[j], text_peer(0, 0, 1))

    def g_at(kind, place):
        return gp.at[SLOT[place]] if kind == 0 else gt.at[2 * SLOT[place]]

    def r_at(kind, i):
        return (rp if kind == 0 else rt).at[i]

    def part(ref, h):
        n = ref.shape[0] // 2
        return ref if h is None else ref.at[pl.ds(h * n, n)]

    def rs_index(i, h):
        return i * 2 + (h if i in (0, 3) else 0)

    def rs_send_to(kind, slot, h, to, i):
        copy(
            part(g_at(kind, slot), h),
            part(r_at(kind, i), h),
            rs_send.at[kind],
            rs_recv.at[kind, rs_index(i, h)],
            peer(kind, *to),
        )

    def rs_add(kind, slot, i, h):
        await_recv(part(r_at(kind, i), h), rs_recv.at[kind, rs_index(i, h)])
        dst, src = part(g_at(kind, slot), h), part(r_at(kind, i), h)
        dst[...] += src[...]

    def sib_add(j):
        await_recv(rsib.at[j], rsib_recv.at[j])
        gt[2 * j] += rsib[j]

    def pass_on(step, kind, h):
        if step == "a":
            rs_send_to(kind, (1, 2), h, PAR, 0)
        elif step == "b1":
            rs_send_to(kind, (1, 1), None, NXT, 1)
        elif step == "b2":
            rs_send_to(kind, (1, 3), None, PRV, 2)
        elif step == "c":
            rs_add(kind, (0, 2), 0, h)
            rs_send_to(kind, (0, 2), h, (PRV, NXT)[h], 3)
        elif step == "d":
            rs_add(kind, (1, 0), 1, None)
            rs_add(kind, (1, 0), 2, None)
            rs_send_to(kind, (1, 0), None, PAR, 4)
        else:
            place = (0, 3) if step in ("e0", "f0") else (0, 1)
            if step in ("f0", "f1"):
                rs_add(kind, place, 3, h)
            rs_send_to(kind, place, h, PRV if place == (0, 3) else NXT, 5 if place == (0, 3) else 6)

    def loss_first():
        own = 0.5 * (rowall[pl.ds(me_p, 1), :] + colall[pl.ds(me_q, 1), :])
        first = lax.broadcasted_iota(jnp.int32, (8, U), 0) == 0
        la[me_p] = jnp.where(first, jnp.broadcast_to(own, (8, U)), 0.0) - macc[...]
        b = la.at[me_p]
        for d in pose_peers:
            copy(b, b, group.at[4], group.at[5], pose_peer(*d))

    def loss_second():
        await_recv(la.at[0:7], group.at[5])
        t = la[0]
        for j in range(1, 8):
            t = t + la[j]
        lb[me_q] = t
        b = lb.at[me_q]
        for d in text_peers:
            copy(b, b, group.at[6], group.at[7], text_peer(*d))

    plan = [
        ("Q", 6, 0), ("a", 0, 0), ("a", 0, 1), ("b1", 0, 0), ("T", 7, 0),
        ("T", 6, 0), ("W", 7, 0), ("a", 1, 0), ("a", 1, 1), ("Q", 4, 0), ("c", 0, 0),
        ("b2", 0, 0), ("W", 6, 0), ("b1", 1, 0), ("T", 5, 0),
        ("T", 4, 0), ("c", 0, 1), ("W", 5, 0), ("b2", 1, 0), ("Q", 2, 0),
        ("W", 4, 0), ("c", 1, 0), ("c", 1, 1), ("f0", 0, 0), ("e0", 0, 1), ("e1", 0, 0),
        ("T", 3, 0), ("f1", 0, 1), ("T", 2, 0), ("W", 3, 0), ("e1", 1, 0), ("T", 1, 0),
        ("W", 2, 0), ("e0", 1, 1), ("L1", 0, 0), ("Q", 0, 0), ("L2", 0, 0), ("d", 0, 0),
        ("W", 1, 0), ("d", 1, 0), ("f0", 1, 0), ("f1", 1, 1), ("T", 0, 0),
        ("W", 0, 0),
    ]
    for step, n, h in plan:
        if step == "Q":
            slope_for(step, n)
            pose_pair(n)
        elif step == "T":
            slope_for(step, n)
            text_pair(n)
        elif step == "W":
            sib_add(n)
        elif step == "L1":
            loss_first()
        elif step == "L2":
            loss_second()
        else:
            pass_on(step, n, h)

    for i in (4, 5, 6):
        rs_add(0, (0, 0), i, None)
    pg_ref[...] = scale * gp[0]
    await_recv(lb.at[0:15], group.at[7])
    t = lb[0]
    for j in range(1, 16):
        t = t + lb[j]
    loss_ref[0, 0] = jnp.sum(t) / (total * LOG2E)
    for i in (4, 5, 6):
        rs_add(1, (0, 0), i, None)
    tg_ref[...] = (scale * gt[0]).T

    for kind in range(2):
        await_recv(xf.at[0:7], ag_send.at[kind])
        await_recv(rp, rs_send.at[kind])
    await_recv(xf, sib_send.at[0])
    await_recv(xf, rsib_send.at[0])
    await_recv(rowrec.at[0:7], group.at[0])
    await_recv(colrec.at[0:15], group.at[2])
    await_recv(la.at[0:7], group.at[4])
    await_recv(lb.at[0:15], group.at[6])


def per_device(pose_emb, text_emb, positive):
    rows, width = pose_emb.shape
    total = rows * lax.axis_size("pose") * lax.axis_size("text")
    scale = 2.0 / math.sqrt(width)
    dma = pltpu.SemaphoreType.DMA
    vmem = pltpu.VMEM
    full = pl.BlockSpec(memory_space=pltpu.VMEM)
    loss, pose_grad, text_grad = pl.pallas_call(
        functools.partial(kernel, scale, total),
        out_shape=(
            jax.ShapeDtypeStruct((1, 1), F32),
            jax.ShapeDtypeStruct((rows, width), F32),
            jax.ShapeDtypeStruct((rows, width), F32),
        ),
        in_specs=[full] * 3,
        out_specs=(pl.BlockSpec(memory_space=pltpu.SMEM), full, full),
        scratch_shapes=[
            vmem((8, U, width), F32),
            vmem((16, U, width), F32),
            vmem((2, 8 * U, width), BF16),
            vmem((2, width, 8 * U), BF16),
            vmem((2, 16 * U, width), BF16),
            vmem((8 * U, 16 * U), F32),
            vmem((2, 8 * U, 16 * U), BF16),
            vmem((8, U, width), F32),
            vmem((16, width, U), F32),
            vmem((7, U, width), F32),
            vmem((7, width, U), F32),
            vmem((8, width, U), F32),
            vmem((8, U, U), F32),
            vmem((8, U, U), F32),
            vmem((8, 16 * U), F32),
            vmem((8, 16 * U), F32),
            vmem((8, U, U), F32),
            vmem((8, U, U), F32),
            vmem((8, 16 * U), F32),
            vmem((16, U), F32),
            vmem((16, U), F32),
            vmem((9, 16, U), F32),
            vmem((17, 16, U), F32),
            vmem((8, 8, U), F32),
            vmem((16, 8, U), F32),
            vmem((8, U), F32),
            dma((2,)),
            dma((2, 16)),
            dma((1,)),
            dma((8,)),
            dma((8,)),
            dma((2,)),
            dma((2, 14)),
            dma((1,)),
            dma((8,)),
        ],
        compiler_params=pltpu.CompilerParams(
            collective_id=0, has_side_effects=True, vmem_limit_bytes=64 * 1024 * 1024 - 64 * 1024
        ),
    )(pose_emb, text_emb, positive.reshape(1, rows))
    return (loss.reshape(()), pose_grad, text_grad)


def solution(mesh):
    return jax.shard_map(
        per_device,
        mesh=mesh,
        in_specs=(P(("pose", "text"), None), P(("pose", "text"), None), P(("pose", "text"))),
        out_specs=(P(), P(("pose", "text"), None), P(("pose", "text"), None)),
        check_vma=False,
    )
```

```python
import functools
import math

import jax
import jax.numpy as jnp
from jax import lax
from jax.experimental import pallas as pl
from jax.experimental.pallas import tpu as pltpu
from jax.sharding import PartitionSpec as P

F32 = jnp.float32
BF16 = jnp.bfloat16
U = 128
H = U // 2
LOG2E = math.log2(math.e)


def split(v):
    hi = v.astype(BF16)
    return hi, (v - hi.astype(F32)).astype(BF16)


def dot_nn(a, b):
    return jnp.dot(a, b, preferred_element_type=F32)


def dot3(ah, al, bh, bl):
    n = ah.shape[0]
    both = dot_nn(jnp.concatenate([ah, al], axis=0), bh)
    return both[:n] + (both[n:] + dot_nn(ah, bl))


ORDER = [(0, 0), (1, 0), (0, 3), (0, 1), (0, 2), (1, 3), (1, 1), (1, 2)]
SLOT = {place: k for k, place in enumerate(ORDER)}
NXT, PRV, PAR = (0, 1), (0, 3), (1, 0)


def kernel(
    scale,
    total,
    pose_ref,
    text_ref,
    pos_ref,
    loss_ref,
    pg_ref,
    tg_ref,
    xf,
    tf,
    xhl,
    xt,
    thl,
    lg,
    sl,
    gp,
    gt,
    rp,
    rt,
    rsib,
    rm,
    rs,
    cm,
    cs,
    rlt,
    idt,
    cv,
    rowst,
    colst,
    rowrec,
    colrec,
    la,
    lb,
    macc,
    ag_send,
    ag_recv,
    sib_send,
    sib_recv,
    group,
    rs_send,
    rs_recv,
    rsib_send,
    rsib_recv,
):
    width = pose_ref.shape[1]
    pi = lax.axis_index("pose")
    ti = lax.axis_index("text")
    yhi, z, core = pi // 8, (pi // 2) % 4, pi % 2
    ylo, x = ti // 4, ti % 4

    def pabs(dy, dx):
        return (ylo + dy) % 2 * 4 + (x + dx) % 4

    def qabs(dy, dz):
        return (yhi + dy) % 2 * 4 + (z + dz) % 4

    def pose_peer(dy, dx):
        return (pi, pabs(dy, dx))

    def text_peer(dy, dz, dc=0):
        return (qabs(dy, dz) * 2 + (core + dc) % 2, (ylo + dy) % 2 * 4 + x)

    pose_peers = [(dy, dx) for dy in range(2) for dx in range(4) if (dy, dx) != (0, 0)]
    text_peers = [
        (dy, dz, dc)
        for dy in range(2)
        for dz in range(4)
        for dc in range(2)
        if (dy, dz, dc) != (0, 0, 0)
    ]

    barrier = pltpu.get_barrier_semaphore()
    near_by = [pose_peer(*d) for d in (NXT, PRV, PAR)]
    near_by += [text_peer(*d) for d in (NXT, PRV, PAR)] + [text_peer(0, 0, 1)]
    for d in near_by:
        pl.semaphore_signal(barrier, inc=1, device_id=d, device_id_type=pl.DeviceIdType.MESH)
    me_p = pabs(0, 0)
    me_q = pi
    xf[me_p] = pose_ref[...]
    tf[me_q] = text_ref[...]
    pl.semaphore_wait(barrier, len(near_by))

    def copy(src, dst, ssem, rsem, dev):
        c = pltpu.make_async_remote_copy(
            src_ref=src,
            dst_ref=dst,
            send_sem=ssem,
            recv_sem=rsem,
            device_id=dev,
            device_id_type=pl.DeviceIdType.MESH,
        )
        c.start()

    def await_recv(dst, rsem):
        pltpu.make_async_copy(dst, dst, rsem).wait()

    def buf(kind, dy, dd, h):
        if kind == 0:
            return xf.at[pabs(dy, dd), pl.ds(h * H, H)]
        return tf.at[qabs(dy, dd) * 2 + core, pl.ds(h * H, H)]

    def peer(kind, dy, dd):
        return pose_peer(dy, dd) if kind == 0 else text_peer(dy, dd, 0)

    def recv_index(place, h):
        return SLOT[place] * 2 + (h if SLOT[place] < 5 else 0)

    def send(kind, src, h, to, arrives):
        b = buf(kind, *src, h)
        copy(b, b, ag_send.at[kind], ag_recv.at[kind, recv_index(arrives, h)], peer(kind, *to))

    def got(kind, place, h):
        await_recv(buf(kind, *place, h), ag_recv.at[kind, SLOT[place] * 2 + h])

    def whole(kind, dy, dd):
        return xf.at[pabs(dy, dd)] if kind == 0 else tf.at[qabs(dy, dd) * 2 + core]

    def got_whole(kind, place):
        await_recv(whole(kind, *place), ag_recv.at[kind, SLOT[place] * 2])

    def share(place):
        b = whole(1, *place)
        copy(b, b, sib_send.at[0], sib_recv.at[SLOT[place]], text_peer(0, 0, 1))

    def got_sib(place):
        await_recv(tf.at[qabs(*place) * 2 + 1 - core], sib_recv.at[SLOT[place]])

    def rows_of(i, n=1):
        return slice(i * U, (i + n) * U)

    def cols_of(j, n=1):
        return slice(j * 2 * U, (j + n) * 2 * U)

    def convert_pose(i):
        v = xf[pabs(*ORDER[i])]
        xhl[0, rows_of(i), :], xhl[1, rows_of(i), :] = split(v)
        xt[0, :, rows_of(i)], xt[1, :, rows_of(i)] = split(v.T)

    def convert_text(j, dc):
        v = tf[qabs(*ORDER[j]) * 2 + (core + dc) % 2]
        rows = rows_of(2 * j + dc)
        thl[0, rows, :], thl[1, rows, :] = split(v)
        sl[0, 0:width, rows], sl[1, 0:width, rows] = split(v.T)

    def stats(i, v, top, total):
        a, b = v[:, 0:U], v[:, U:]
        old = rm[i]
        new = jnp.maximum(jnp.maximum(a, b), old)
        rs[i] = rs[i] * jnp.exp2(old - new) + jnp.exp2(a - new) + jnp.exp2(b - new)
        rm[i] = new
        w = v.reshape(U // 8, 8, 2 * U)
        new = jnp.maximum(top, jnp.max(w, axis=0))
        return new, total * jnp.exp2(top - new) + jnp.sum(jnp.exp2(w - new[None]), axis=0)

    def logits(i, n, j, count=1):
        def body(jj):
            c = pl.ds(pl.multiple_of(jj * 2 * U, 2 * U), 2 * U)
            th, tl = sl[0, 0:width, c], sl[1, 0:width, c]
            top, total = cm[:, c], cs[:, c]
            k = i
            while k < i + n:
                m = min(2, i + n - k)
                r = rows_of(k, m)
                xh, xl = xhl[0, r, :], xhl[1, r, :]
                v = (scale * LOG2E) * dot3(xh, xl, th, tl)
                lg[r, c] = v
                for q in range(m):
                    top, total = stats(k + q, v[rows_of(q)], top, total)
                k += m
            cm[:, c], cs[:, c] = top, total

        if count == 1:
            body(j)
        else:

            def step(jj, carry):
                body(jj)
                return carry

            lax.fori_loop(j, j + count, step, 0)

    for ref in (rm, cm):
        ref[...] = jnp.full_like(ref, -jnp.inf)
    for ref in (rs, cs):
        ref[...] = jnp.zeros_like(ref)

    for h in range(2):
        for kind in range(2):
            send(kind, (0, 0), h, NXT, (0, 3))
            send(kind, (0, 0), 1 - h, PRV, (0, 1))
            send(kind, (0, 0), h, PAR, (1, 0))
    share((0, 0))
    convert_pose(0)
    convert_text(0, 0)

    for kind in range(2):
        got(kind, (0, 3), 0)
        send(kind, (0, 3), 0, NXT, (0, 2))
        got(kind, (0, 1), 1)
        send(kind, (0, 1), 1, PRV, (0, 2))
    for kind in range(2):
        got(kind, (1, 0), 0)
        send(kind, (1, 0), 0, NXT, (1, 3))
        send(kind, (1, 0), 0, PRV, (1, 1))
    got_sib((0, 0))
    convert_text(0, 1)
    for kind in range(2):
        got(kind, (0, 3), 1)
        got(kind, (0, 1), 0)
    for kind in range(2):
        got(kind, (1, 0), 1)
        send(kind, (1, 0), 1, NXT, (1, 3))
        send(kind, (1, 0), 1, PRV, (1, 1))
    for i in (1, 2, 3):
        share(ORDER[i])
    for i in (1, 2, 3):
        convert_pose(i)
        convert_text(i, 0)
    for j in (1, 2, 3):
        got_sib(ORDER[j])
        convert_text(j, 1)
    logits(0, 4, 0, 4)
    for h in range(2):
        for kind in range(2):
            got(kind, (0, 2), h)
            send(kind, (0, 2), h, PAR, (1, 2))
    share((0, 2))
    convert_pose(4)
    convert_text(4, 0)
    got_sib((0, 2))
    convert_text(4, 1)
    logits(4, 1, 0, 4)
    logits(0, 5, 4)
    for i in (5, 6):
        got_whole(0, ORDER[i])
        convert_pose(i)
    for i in (5, 6):
        got_whole(1, ORDER[i])
        share(ORDER[i])
        convert_text(i, 0)
    logits(5, 2, 0, 5)
    for j in (5, 6):
        got_sib(ORDER[j])
        convert_text(j, 1)
    logits(0, 7, 5, 2)
    for kind in range(2):
        got_whole(kind, (1, 2))
    share((1, 2))
    convert_pose(7)
    convert_text(7, 0)
    logits(7, 1, 0, 7)
    got_sib((1, 2))
    convert_text(7, 1)
    logits(0, 8, 7)

    for i in range(8):
        mt, st = rm[i].T, rs[i].T
        m = jnp.max(mt, axis=0, keepdims=True)
        s = jnp.sum(st * jnp.exp2(mt - m), axis=0, keepdims=True)
        rowst[pl.ds(pabs(*ORDER[i]), 1), :] = m + jnp.log2(s)
    rowst[8:16, :] = jnp.broadcast_to(pos_ref[...].astype(F32), (8, U))
    m = jnp.max(cm[...], axis=0, keepdims=True)
    s = jnp.sum(cs[...] * jnp.exp2(cm[...] - m), axis=0, keepdims=True)
    lse = m + jnp.log2(s)
    for j in range(8):
        for dc in range(2):
            p = qabs(*ORDER[j]) * 2 + (core + dc) % 2
            colst[pl.ds(p, 1), :] = lse[:, rows_of(2 * j + dc)]

    for d in pose_peers:
        copy(rowst, rowrec.at[me_p], group.at[0], group.at[1], pose_peer(*d))
    for d in text_peers:
        copy(colst, colrec.at[me_q], group.at[2], group.at[3], text_peer(*d))
    rowrec[me_p] = rowst[...]
    colrec[me_q] = colst[...]
    await_recv(rowrec.at[0:7], group.at[1])
    await_recv(colrec.at[0:15], group.at[3])

    def lse_of(parts):
        m = parts[0]
        for p in parts[1:]:
            m = jnp.maximum(m, p)
        s = jnp.exp2(parts[0] - m)
        for p in parts[1:]:
            s = s + jnp.exp2(p - m)
        return m + jnp.log2(s)

    rowall, colall = rowrec.at[8], colrec.at[16]
    rowall[0:8] = lse_of([rowrec[k, 0:8, :] for k in range(8)])
    colall[...] = lse_of([colrec[k] for k in range(16)])
    for i in range(8):
        a = pabs(*ORDER[i])
        rlt[i] = jnp.broadcast_to(rowall[pl.ds(a, 1), :] + 1.0, (U, U)).T
        idt[i] = jnp.broadcast_to(rowrec[a, 8:9, :], (U, U)).T

    macc[...] = jnp.zeros_like(macc)
    lane = lax.broadcasted_iota(jnp.int32, (1, U), 1)
    for j, (dy, dz) in enumerate(ORDER):
        for dc in range(2):
            p = qabs(dy, dz) * 2 + (core + dc) % 2
            base = (p * 8 + (ylo + dy) % 2 * 4 + x) * U
            cv[0:1, rows_of(2 * j + dc)] = colall[pl.ds(p, 1), :] + 1.0
            cv[1:2, rows_of(2 * j + dc)] = (base + lane).astype(F32)

    def loop(lo, hi, body):
        def step(k, carry):
            body(k)
            return carry

        if hi > lo:
            lax.fori_loop(lo, hi, step, 0)

    def slope(i2, j):
        acc = None
        for u in range(2):
            rl, ids = rlt[2 * i2 + u], idt[2 * i2 + u]
            r = pl.ds(pl.multiple_of((2 * i2 + u) * U, U), U)
            for dc in range(2):
                c = pl.ds(pl.multiple_of((2 * j + dc) * U, U), U)
                v = lg[r, c]
                hit = ids == cv[1:2, c]
                g = jnp.exp2(v - rl) + jnp.exp2(v - cv[0:1, c])
                t = jnp.where(hit, v, 0.0)
                acc = t if acc is None else acc + t
                hi, lo = split(jnp.where(hit, g - 1.0, g))
                sl[0, r, c] = hi
                sl[1, r, c] = lo
        macc[...] += jnp.sum(acc.reshape(U // 8, 8, U), axis=0)

    reach = {"wide": 8, "tall": 8}

    def slope_for(step, n):
        if step == "Q":
            loop(0, reach["wide"], lambda j: slope(n // 2, j))
            reach["tall"] = n
        else:
            new = min(n, reach["wide"])
            if new < reach["wide"]:
                for j in range(new, reach["wide"]):
                    loop(0, reach["tall"] // 2, lambda i2, j=j: slope(i2, j))
                reach["wide"] = new

    def pose_pair(i):
        r = rows_of(i, 2)

        def body(k):
            c = pl.ds(pl.multiple_of(k * 2 * U, 2 * U), 2 * U)
            sh, sw = sl[0, r, :], sl[1, r, :]
            th = thl[0, :, c]
            g = dot3(sh, sw, th, thl[1, :, c])
            gp[i, :, c] = g[0:U]
            gp[i + 1, :, c] = g[U:]

        loop(0, width // (2 * U), body)

    def text_pair(j):
        c = cols_of(j)

        def body(k):
            r = pl.ds(pl.multiple_of(k * 2 * U, 2 * U), 2 * U)
            sh, sw = sl[0, :, c], sl[1, :, c]
            xh = xt[0, r, :]
            g = dot3(xh, xt[1, r, :], sh, sw)
            gt[2 * j, r, :] = g[:, 0:U]
            gt[2 * j + 1, r, :] = g[:, U:]

        loop(0, width // (2 * U), body)
        copy(gt.at[2 * j + 1], rsib.at[j], rsib_send.at[0], rsib_recv.at[j], text_peer(0, 0, 1))

    def g_at(kind, place):
        return gp.at[SLOT[place]] if kind == 0 else gt.at[2 * SLOT[place]]

    def r_at(kind, i):
        return (rp if kind == 0 else rt).at[i]

    def part(ref, h):
        n = ref.shape[0] // 2
        return ref if h is None else ref.at[pl.ds(h * n, n)]

    def rs_index(i, h):
        return i * 2 + (h if i in (0, 3) else 0)

    def rs_send_to(kind, slot, h, to, i):
        copy(
            part(g_at(kind, slot), h),
            part(r_at(kind, i), h),
            rs_send.at[kind],
            rs_recv.at[kind, rs_index(i, h)],
            peer(kind, *to),
        )

    def rs_add(kind, slot, i, h):
        await_recv(part(r_at(kind, i), h), rs_recv.at[kind, rs_index(i, h)])
        dst, src = part(g_at(kind, slot), h), part(r_at(kind, i), h)
        dst[...] += src[...]

    def sib_add(j):
        await_recv(rsib.at[j], rsib_recv.at[j])
        gt[2 * j] += rsib[j]

    def pass_on(step, kind, h):
        if step == "a":
            rs_send_to(kind, (1, 2), h, PAR, 0)
        elif step == "b1":
            rs_send_to(kind, (1, 1), None, NXT, 1)
        elif step == "b2":
            rs_send_to(kind, (1, 3), None, PRV, 2)
        elif step == "c":
            rs_add(kind, (0, 2), 0, h)
            rs_send_to(kind, (0, 2), h, (PRV, NXT)[h], 3)
        elif step == "d":
            rs_add(kind, (1, 0), 1, None)
            rs_add(kind, (1, 0), 2, None)
            rs_send_to(kind, (1, 0), None, PAR, 4)
        else:
            place = (0, 3) if step in ("e0", "f0") else (0, 1)
            if step in ("f0", "f1"):
                rs_add(kind, place, 3, h)
            rs_send_to(kind, place, h, PRV if place == (0, 3) else NXT, 5 if place == (0, 3) else 6)

    def loss_first():
        own = 0.5 * (rowall[pl.ds(me_p, 1), :] + colall[pl.ds(me_q, 1), :])
        first = lax.broadcasted_iota(jnp.int32, (8, U), 0) == 0
        la[me_p] = jnp.where(first, jnp.broadcast_to(own, (8, U)), 0.0) - macc[...]
        b = la.at[me_p]
        for d in pose_peers:
            copy(b, b, group.at[4], group.at[5], pose_peer(*d))

    def loss_second():
        await_recv(la.at[0:7], group.at[5])
        t = la[0]
        for j in range(1, 8):
            t = t + la[j]
        lb[me_q] = t
        b = lb.at[me_q]
        for d in text_peers:
            copy(b, b, group.at[6], group.at[7], text_peer(*d))

    plan = [
        ("Q", 6, 0), ("a", 0, 0), ("a", 0, 1), ("b1", 0, 0), ("T", 7, 0),
        ("T", 6, 0), ("W", 7, 0), ("a", 1, 0), ("a", 1, 1), ("Q", 4, 0), ("c", 0, 0),
        ("b2", 0, 0), ("W", 6, 0), ("b1", 1, 0), ("T", 5, 0),
        ("T", 4, 0), ("c", 0, 1), ("W", 5, 0), ("b2", 1, 0), ("Q", 2, 0),
        ("W", 4, 0), ("c", 1, 0), ("c", 1, 1), ("f0", 0, 0), ("e0", 0, 1), ("e1", 0, 0),
        ("T", 3, 0), ("f1", 0, 1), ("T", 2, 0), ("W", 3, 0), ("e1", 1, 0), ("T", 1, 0),
        ("W", 2, 0), ("e0", 1, 1), ("Q", 0, 0), ("L1", 0, 0), ("d", 0, 0),
        ("W", 1, 0), ("d", 1, 0), ("f0", 1, 0), ("f1", 1, 1), ("T", 0, 0),
        ("W", 0, 0), ("L2", 0, 0),
    ]
    for step, n, h in plan:
        if step == "Q":
            slope_for(step, n)
            pose_pair(n)
        elif step == "T":
            slope_for(step, n)
            text_pair(n)
        elif step == "W":
            sib_add(n)
        elif step == "L1":
            loss_first()
        elif step == "L2":
            loss_second()
        else:
            pass_on(step, n, h)

    for i in (4, 5, 6):
        rs_add(0, (0, 0), i, None)
    pg_ref[...] = scale * gp[0]
    await_recv(lb.at[0:15], group.at[7])
    t = lb[0]
    for j in range(1, 16):
        t = t + lb[j]
    loss_ref[0, 0] = jnp.sum(t) / (total * LOG2E)
    for i in (4, 5, 6):
        rs_add(1, (0, 0), i, None)
    tg_ref[...] = (scale * gt[0]).T

    for kind in range(2):
        await_recv(xf.at[0:7], ag_send.at[kind])
        await_recv(rp, rs_send.at[kind])
    await_recv(xf, sib_send.at[0])
    await_recv(xf, rsib_send.at[0])
    await_recv(rowrec.at[0:7], group.at[0])
    await_recv(colrec.at[0:15], group.at[2])
    await_recv(la.at[0:7], group.at[4])
    await_recv(lb.at[0:15], group.at[6])


def per_device(pose_emb, text_emb, positive):
    rows, width = pose_emb.shape
    total = rows * lax.axis_size("pose") * lax.axis_size("text")
    scale = 2.0 / math.sqrt(width)
    dma = pltpu.SemaphoreType.DMA
    vmem = pltpu.VMEM
    full = pl.BlockSpec(memory_space=pltpu.VMEM)
    loss, pose_grad, text_grad = pl.pallas_call(
        functools.partial(kernel, scale, total),
        out_shape=(
            jax.ShapeDtypeStruct((1, 1), F32),
            jax.ShapeDtypeStruct((rows, width), F32),
            jax.ShapeDtypeStruct((rows, width), F32),
        ),
        in_specs=[full] * 3,
        out_specs=(pl.BlockSpec(memory_space=pltpu.SMEM), full, full),
        scratch_shapes=[
            vmem((8, U, width), F32),
            vmem((16, U, width), F32),
            vmem((2, 8 * U, width), BF16),
            vmem((2, width, 8 * U), BF16),
            vmem((2, 16 * U, width), BF16),
            vmem((8 * U, 16 * U), F32),
            vmem((2, 8 * U, 16 * U), BF16),
            vmem((8, U, width), F32),
            vmem((16, width, U), F32),
            vmem((7, U, width), F32),
            vmem((7, width, U), F32),
            vmem((8, width, U), F32),
            vmem((8, U, U), F32),
            vmem((8, U, U), F32),
            vmem((8, 16 * U), F32),
            vmem((8, 16 * U), F32),
            vmem((8, U, U), F32),
            vmem((8, U, U), F32),
            vmem((8, 16 * U), F32),
            vmem((16, U), F32),
            vmem((16, U), F32),
            vmem((9, 16, U), F32),
            vmem((17, 16, U), F32),
            vmem((8, 8, U), F32),
            vmem((16, 8, U), F32),
            vmem((8, U), F32),
            dma((2,)),
            dma((2, 16)),
            dma((1,)),
            dma((8,)),
            dma((8,)),
            dma((2,)),
            dma((2, 14)),
            dma((1,)),
            dma((8,)),
        ],
        compiler_params=pltpu.CompilerParams(
            collective_id=0, has_side_effects=True, vmem_limit_bytes=64 * 1024 * 1024 - 64 * 1024
        ),
    )(pose_emb, text_emb, positive.reshape(1, rows))
    return (loss.reshape(()), pose_grad, text_grad)


def solution(mesh):
    return jax.shard_map(
        per_device,
        mesh=mesh,
        in_specs=(P(("pose", "text"), None), P(("pose", "text"), None), P(("pose", "text"))),
        out_specs=(P(), P(("pose", "text"), None), P(("pose", "text"), None)),
        check_vma=False,
    )
```

```python
import functools
import math

import jax
import jax.numpy as jnp
from jax import lax
from jax.experimental import pallas as pl
from jax.experimental.pallas import tpu as pltpu
from jax.sharding import PartitionSpec as P

F32 = jnp.float32
BF16 = jnp.bfloat16
U = 128
H = U // 2
LOG2E = math.log2(math.e)


def split(v):
    hi = v.astype(BF16)
    return hi, (v - hi.astype(F32)).astype(BF16)


def dot_nn(a, b):
    return jnp.dot(a, b, preferred_element_type=F32)


def dot3(ah, al, bh, bl):
    n = ah.shape[0]
    both = dot_nn(jnp.concatenate([ah, al], axis=0), bh)
    return both[:n] + (both[n:] + dot_nn(ah, bl))


ORDER = [(0, 0), (0, 3), (0, 1), (1, 0), (0, 2), (1, 3), (1, 1), (1, 2)]
SLOT = {place: k for k, place in enumerate(ORDER)}
NXT, PRV, PAR = (0, 1), (0, 3), (1, 0)


def kernel(
    scale,
    total,
    pose_ref,
    text_ref,
    pos_ref,
    loss_ref,
    pg_ref,
    tg_ref,
    xf,
    tf,
    xhl,
    xt,
    thl,
    lg,
    sl,
    gp,
    gt,
    rp,
    rt,
    rsib,
    rm,
    rs,
    cm,
    cs,
    rlt,
    idt,
    cv,
    rowst,
    colst,
    rowrec,
    colrec,
    la,
    lb,
    macc,
    ag_send,
    ag_recv,
    sib_send,
    sib_recv,
    group,
    rs_send,
    rs_recv,
    rsib_send,
    rsib_recv,
):
    width = pose_ref.shape[1]
    pi = lax.axis_index("pose")
    ti = lax.axis_index("text")
    yhi, z, core = pi // 8, (pi // 2) % 4, pi % 2
    ylo, x = ti // 4, ti % 4

    def pabs(dy, dx):
        return (ylo + dy) % 2 * 4 + (x + dx) % 4

    def qabs(dy, dz):
        return (yhi + dy) % 2 * 4 + (z + dz) % 4

    def pose_peer(dy, dx):
        return (pi, pabs(dy, dx))

    def text_peer(dy, dz, dc=0):
        return (qabs(dy, dz) * 2 + (core + dc) % 2, (ylo + dy) % 2 * 4 + x)

    pose_peers = [(dy, dx) for dy in range(2) for dx in range(4) if (dy, dx) != (0, 0)]
    text_peers = [
        (dy, dz, dc)
        for dy in range(2)
        for dz in range(4)
        for dc in range(2)
        if (dy, dz, dc) != (0, 0, 0)
    ]

    barrier = pltpu.get_barrier_semaphore()
    near_by = [pose_peer(*d) for d in (NXT, PRV, PAR)]
    near_by += [text_peer(*d) for d in (NXT, PRV, PAR)] + [text_peer(0, 0, 1)]
    for d in near_by:
        pl.semaphore_signal(barrier, inc=1, device_id=d, device_id_type=pl.DeviceIdType.MESH)
    me_p = pabs(0, 0)
    me_q = pi
    xf[me_p] = pose_ref[...]
    tf[me_q] = text_ref[...]
    pl.semaphore_wait(barrier, len(near_by))

    def copy(src, dst, ssem, rsem, dev):
        c = pltpu.make_async_remote_copy(
            src_ref=src,
            dst_ref=dst,
            send_sem=ssem,
            recv_sem=rsem,
            device_id=dev,
            device_id_type=pl.DeviceIdType.MESH,
        )
        c.start()

    def await_recv(dst, rsem):
        pltpu.make_async_copy(dst, dst, rsem).wait()

    def buf(kind, dy, dd, h):
        if kind == 0:
            return xf.at[pabs(dy, dd), pl.ds(h * H, H)]
        return tf.at[qabs(dy, dd) * 2 + core, pl.ds(h * H, H)]

    def peer(kind, dy, dd):
        return pose_peer(dy, dd) if kind == 0 else text_peer(dy, dd, 0)

    def recv_index(place, h):
        return SLOT[place] * 2 + (h if SLOT[place] < 5 else 0)

    def send(kind, src, h, to, arrives):
        b = buf(kind, *src, h)
        copy(b, b, ag_send.at[kind], ag_recv.at[kind, recv_index(arrives, h)], peer(kind, *to))

    def got(kind, place, h):
        await_recv(buf(kind, *place, h), ag_recv.at[kind, SLOT[place] * 2 + h])

    def whole(kind, dy, dd):
        return xf.at[pabs(dy, dd)] if kind == 0 else tf.at[qabs(dy, dd) * 2 + core]

    def got_whole(kind, place):
        await_recv(whole(kind, *place), ag_recv.at[kind, SLOT[place] * 2])

    def share(place):
        b = whole(1, *place)
        copy(b, b, sib_send.at[0], sib_recv.at[SLOT[place]], text_peer(0, 0, 1))

    def got_sib(place):
        await_recv(tf.at[qabs(*place) * 2 + 1 - core], sib_recv.at[SLOT[place]])

    def rows_of(i, n=1):
        return slice(i * U, (i + n) * U)

    def cols_of(j, n=1):
        return slice(j * 2 * U, (j + n) * 2 * U)

    def convert_pose(i):
        v = xf[pabs(*ORDER[i])]
        xhl[0, rows_of(i), :], xhl[1, rows_of(i), :] = split(v)
        xt[0, :, rows_of(i)], xt[1, :, rows_of(i)] = split(v.T)

    def convert_text(j, dc):
        v = tf[qabs(*ORDER[j]) * 2 + (core + dc) % 2]
        rows = rows_of(2 * j + dc)
        thl[0, rows, :], thl[1, rows, :] = split(v)
        sl[0, 0:width, rows], sl[1, 0:width, rows] = split(v.T)

    def stats(i, v, top, total):
        a, b = v[:, 0:U], v[:, U:]
        old = rm[i]
        new = jnp.maximum(jnp.maximum(a, b), old)
        rs[i] = rs[i] * jnp.exp2(old - new) + jnp.exp2(a - new) + jnp.exp2(b - new)
        rm[i] = new
        w = v.reshape(U // 8, 8, 2 * U)
        new = jnp.maximum(top, jnp.max(w, axis=0))
        return new, total * jnp.exp2(top - new) + jnp.sum(jnp.exp2(w - new[None]), axis=0)

    def logits(i, n, j, count=1):
        def body(jj):
            c = pl.ds(pl.multiple_of(jj * 2 * U, 2 * U), 2 * U)
            th, tl = sl[0, 0:width, c], sl[1, 0:width, c]
            top, total = cm[:, c], cs[:, c]
            k = i
            while k < i + n:
                m = min(2, i + n - k)
                r = rows_of(k, m)
                xh, xl = xhl[0, r, :], xhl[1, r, :]
                v = (scale * LOG2E) * dot3(xh, xl, th, tl)
                lg[r, c] = v
                for q in range(m):
                    top, total = stats(k + q, v[rows_of(q)], top, total)
                k += m
            cm[:, c], cs[:, c] = top, total

        if count == 1:
            body(j)
        else:

            def step(jj, carry):
                body(jj)
                return carry

            lax.fori_loop(j, j + count, step, 0)

    for ref in (rm, cm):
        ref[...] = jnp.full_like(ref, -jnp.inf)
    for ref in (rs, cs):
        ref[...] = jnp.zeros_like(ref)

    for h in range(2):
        for kind in range(2):
            send(kind, (0, 0), h, NXT, (0, 3))
            send(kind, (0, 0), 1 - h, PRV, (0, 1))
            send(kind, (0, 0), h, PAR, (1, 0))
    share((0, 0))
    convert_pose(0)
    convert_text(0, 0)

    for kind in range(2):
        got(kind, (0, 3), 0)
        send(kind, (0, 3), 0, NXT, (0, 2))
        got(kind, (0, 1), 1)
        send(kind, (0, 1), 1, PRV, (0, 2))
    for kind in range(2):
        got(kind, (1, 0), 0)
        send(kind, (1, 0), 0, NXT, (1, 3))
        send(kind, (1, 0), 0, PRV, (1, 1))
    got_sib((0, 0))
    convert_text(0, 1)
    for kind in range(2):
        got(kind, (0, 3), 1)
        got(kind, (0, 1), 0)
    for kind in range(2):
        got(kind, (1, 0), 1)
        send(kind, (1, 0), 1, NXT, (1, 3))
        send(kind, (1, 0), 1, PRV, (1, 1))
    for i in (1, 2, 3):
        share(ORDER[i])
    for i in (1, 2, 3):
        convert_pose(i)
        convert_text(i, 0)
    for j in (1, 2, 3):
        got_sib(ORDER[j])
        convert_text(j, 1)
    logits(0, 4, 0, 2)
    for h in range(2):
        for kind in range(2):
            got(kind, (0, 2), h)
            send(kind, (0, 2), h, PAR, (1, 2))
    share((0, 2))
    logits(0, 4, 2, 2)
    convert_pose(4)
    convert_text(4, 0)
    got_sib((0, 2))
    convert_text(4, 1)
    logits(4, 1, 0, 4)
    logits(0, 5, 4)
    for i in (5, 6):
        got_whole(0, ORDER[i])
        convert_pose(i)
    for i in (5, 6):
        got_whole(1, ORDER[i])
        share(ORDER[i])
        convert_text(i, 0)
    logits(5, 2, 0, 5)
    for j in (5, 6):
        got_sib(ORDER[j])
        convert_text(j, 1)
    logits(0, 7, 5, 2)
    for kind in range(2):
        got_whole(kind, (1, 2))
    share((1, 2))
    convert_pose(7)
    convert_text(7, 0)
    logits(7, 1, 0, 7)
    got_sib((1, 2))
    convert_text(7, 1)
    logits(0, 8, 7)

    for i in range(8):
        mt, st = rm[i].T, rs[i].T
        m = jnp.max(mt, axis=0, keepdims=True)
        s = jnp.sum(st * jnp.exp2(mt - m), axis=0, keepdims=True)
        rowst[pl.ds(pabs(*ORDER[i]), 1), :] = m + jnp.log2(s)
    rowst[8:16, :] = jnp.broadcast_to(pos_ref[...].astype(F32), (8, U))
    m = jnp.max(cm[...], axis=0, keepdims=True)
    s = jnp.sum(cs[...] * jnp.exp2(cm[...] - m), axis=0, keepdims=True)
    lse = m + jnp.log2(s)
    for j in range(8):
        for dc in range(2):
            p = qabs(*ORDER[j]) * 2 + (core + dc) % 2
            colst[pl.ds(p, 1), :] = lse[:, rows_of(2 * j + dc)]

    for d in pose_peers:
        copy(rowst, rowrec.at[me_p], group.at[0], group.at[1], pose_peer(*d))
    for d in text_peers:
        copy(colst, colrec.at[me_q], group.at[2], group.at[3], text_peer(*d))
    rowrec[me_p] = rowst[...]
    colrec[me_q] = colst[...]
    await_recv(rowrec.at[0:7], group.at[1])
    await_recv(colrec.at[0:15], group.at[3])

    def lse_of(parts):
        m = parts[0]
        for p in parts[1:]:
            m = jnp.maximum(m, p)
        s = jnp.exp2(parts[0] - m)
        for p in parts[1:]:
            s = s + jnp.exp2(p - m)
        return m + jnp.log2(s)

    rowall, colall = rowrec.at[8], colrec.at[16]
    rowall[0:8] = lse_of([rowrec[k, 0:8, :] for k in range(8)])
    colall[...] = lse_of([colrec[k] for k in range(16)])
    for i in range(8):
        a = pabs(*ORDER[i])
        rlt[i] = jnp.broadcast_to(rowall[pl.ds(a, 1), :] + 1.0, (U, U)).T
        idt[i] = jnp.broadcast_to(rowrec[a, 8:9, :], (U, U)).T

    macc[...] = jnp.zeros_like(macc)
    lane = lax.broadcasted_iota(jnp.int32, (1, U), 1)
    for j, (dy, dz) in enumerate(ORDER):
        for dc in range(2):
            p = qabs(dy, dz) * 2 + (core + dc) % 2
            base = (p * 8 + (ylo + dy) % 2 * 4 + x) * U
            cv[0:1, rows_of(2 * j + dc)] = colall[pl.ds(p, 1), :] + 1.0
            cv[1:2, rows_of(2 * j + dc)] = (base + lane).astype(F32)

    def loop(lo, hi, body):
        def step(k, carry):
            body(k)
            return carry

        if hi > lo:
            lax.fori_loop(lo, hi, step, 0)

    def slope(i2, j):
        acc = None
        for u in range(2):
            rl, ids = rlt[2 * i2 + u], idt[2 * i2 + u]
            r = pl.ds(pl.multiple_of((2 * i2 + u) * U, U), U)
            for dc in range(2):
                c = pl.ds(pl.multiple_of((2 * j + dc) * U, U), U)
                v = lg[r, c]
                hit = ids == cv[1:2, c]
                g = jnp.exp2(v - rl) + jnp.exp2(v - cv[0:1, c])
                t = jnp.where(hit, v, 0.0)
                acc = t if acc is None else acc + t
                hi, lo = split(jnp.where(hit, g - 1.0, g))
                sl[0, r, c] = hi
                sl[1, r, c] = lo
        macc[...] += jnp.sum(acc.reshape(U // 8, 8, U), axis=0)

    reach = {"wide": 8, "tall": 8}

    def slope_for(step, n):
        if step != "T":
            pair = {6: 3, 4: 2, 3: 1, 1: 0}.get(n)
            if pair is not None:
                loop(0, reach["wide"], lambda j: slope(pair, j))
                reach["tall"] = 2 * pair
        else:
            new = min(n, reach["wide"])
            if new < reach["wide"]:
                for j in range(new, reach["wide"]):
                    loop(0, reach["tall"] // 2, lambda i2, j=j: slope(i2, j))
                reach["wide"] = new

    def pose_rows(i, n):
        r = rows_of(i, n)

        def body(k):
            c = pl.ds(pl.multiple_of(k * 2 * U, 2 * U), 2 * U)
            sh, sw = sl[0, r, :], sl[1, r, :]
            th = thl[0, :, c]
            g = dot3(sh, sw, th, thl[1, :, c])
            for u in range(n):
                gp[i + u, :, c] = g[rows_of(u)]

        loop(0, width // (2 * U), body)

    def text_pair(j):
        c = cols_of(j)

        def body(k):
            r = pl.ds(pl.multiple_of(k * 2 * U, 2 * U), 2 * U)
            sh, sw = sl[0, :, c], sl[1, :, c]
            xh = xt[0, r, :]
            g = dot3(xh, xt[1, r, :], sh, sw)
            gt[2 * j, r, :] = g[:, 0:U]
            gt[2 * j + 1, r, :] = g[:, U:]

        loop(0, width // (2 * U), body)
        copy(gt.at[2 * j + 1], rsib.at[j], rsib_send.at[0], rsib_recv.at[j], text_peer(0, 0, 1))

    def g_at(kind, place):
        return gp.at[SLOT[place]] if kind == 0 else gt.at[2 * SLOT[place]]

    def r_at(kind, i):
        return (rp if kind == 0 else rt).at[i]

    def part(ref, h):
        n = ref.shape[0] // 2
        return ref if h is None else ref.at[pl.ds(h * n, n)]

    def rs_index(i, h):
        return i * 2 + (h if i in (0, 3) else 0)

    def rs_send_to(kind, slot, h, to, i):
        copy(
            part(g_at(kind, slot), h),
            part(r_at(kind, i), h),
            rs_send.at[kind],
            rs_recv.at[kind, rs_index(i, h)],
            peer(kind, *to),
        )

    def rs_add(kind, slot, i, h):
        await_recv(part(r_at(kind, i), h), rs_recv.at[kind, rs_index(i, h)])
        dst, src = part(g_at(kind, slot), h), part(r_at(kind, i), h)
        dst[...] += src[...]

    def sib_add(j):
        await_recv(rsib.at[j], rsib_recv.at[j])
        gt[2 * j] += rsib[j]

    def pass_on(step, kind, h):
        if step == "a":
            rs_send_to(kind, (1, 2), h, PAR, 0)
        elif step == "b1":
            rs_send_to(kind, (1, 1), None, NXT, 1)
        elif step == "b2":
            rs_send_to(kind, (1, 3), None, PRV, 2)
        elif step == "c":
            rs_add(kind, (0, 2), 0, h)
            rs_send_to(kind, (0, 2), h, (PRV, NXT)[h], 3)
        elif step == "d":
            rs_add(kind, (1, 0), 1, None)
            rs_add(kind, (1, 0), 2, None)
            rs_send_to(kind, (1, 0), None, PAR, 4)
        else:
            place = (0, 3) if step in ("e0", "f0") else (0, 1)
            if step in ("f0", "f1"):
                rs_add(kind, place, 3, h)
            rs_send_to(kind, place, h, PRV if place == (0, 3) else NXT, 5 if place == (0, 3) else 6)

    def loss_first():
        own = 0.5 * (rowall[pl.ds(me_p, 1), :] + colall[pl.ds(me_q, 1), :])
        first = lax.broadcasted_iota(jnp.int32, (8, U), 0) == 0
        la[me_p] = jnp.where(first, jnp.broadcast_to(own, (8, U)), 0.0) - macc[...]
        b = la.at[me_p]
        for d in pose_peers:
            copy(b, b, group.at[4], group.at[5], pose_peer(*d))

    def loss_second():
        await_recv(la.at[0:7], group.at[5])
        t = la[0]
        for j in range(1, 8):
            t = t + la[j]
        lb[me_q] = t
        b = lb.at[me_q]
        for d in text_peers:
            copy(b, b, group.at[6], group.at[7], text_peer(*d))

    plan = [
        ("T", 7, 0), ("Q", 6, 0), ("a", 0, 0), ("a", 0, 1), ("W", 7, 0), ("a", 1, 0),
        ("a", 1, 1), ("b1", 0, 0), ("Q", 4, 0), ("b2", 0, 0), ("T", 6, 0), ("c", 0, 0),
        ("T", 5, 0), ("W", 6, 0), ("b1", 1, 0), ("T", 4, 0), ("c", 0, 1), ("W", 5, 0),
        ("b2", 1, 0), ("T", 3, 0), ("W", 4, 0), ("c", 1, 0), ("c", 1, 1), ("T", 2, 0),
        ("T", 1, 0), ("W", 2, 0), ("e1", 1, 0), ("P", 3, 0), ("d", 0, 0), ("W", 1, 0),
        ("e0", 1, 1), ("Q", 1, 0), ("L1", 0, 0), ("W", 3, 0), ("d", 1, 0), ("f0", 0, 0),
        ("f1", 0, 1), ("f1", 1, 1), ("e0", 0, 1), ("e1", 0, 0), ("P", 0, 0), ("f0", 1, 0),
        ("T", 0, 0), ("W", 0, 0), ("L2", 0, 0),
    ]
    for step, n, h in plan:
        if step in ("Q", "P"):
            slope_for(step, n)
            pose_rows(n, 2 if step == "Q" else 1)
        elif step == "T":
            slope_for(step, n)
            text_pair(n)
        elif step == "W":
            sib_add(n)
        elif step == "L1":
            loss_first()
        elif step == "L2":
            loss_second()
        else:
            pass_on(step, n, h)

    for i in (4, 5, 6):
        rs_add(0, (0, 0), i, None)
    pg_ref[...] = scale * gp[0]
    await_recv(lb.at[0:15], group.at[7])
    t = lb[0]
    for j in range(1, 16):
        t = t + lb[j]
    loss_ref[0, 0] = jnp.sum(t) / (total * LOG2E)
    for i in (4, 5, 6):
        rs_add(1, (0, 0), i, None)
    tg_ref[...] = (scale * gt[0]).T

    for kind in range(2):
        await_recv(xf.at[0:7], ag_send.at[kind])
        await_recv(rp, rs_send.at[kind])
    await_recv(xf, sib_send.at[0])
    await_recv(xf, rsib_send.at[0])
    await_recv(rowrec.at[0:7], group.at[0])
    await_recv(colrec.at[0:15], group.at[2])
    await_recv(la.at[0:7], group.at[4])
    await_recv(lb.at[0:15], group.at[6])


def per_device(pose_emb, text_emb, positive):
    rows, width = pose_emb.shape
    total = rows * lax.axis_size("pose") * lax.axis_size("text")
    scale = 2.0 / math.sqrt(width)
    dma = pltpu.SemaphoreType.DMA
    vmem = pltpu.VMEM
    full = pl.BlockSpec(memory_space=pltpu.VMEM)
    loss, pose_grad, text_grad = pl.pallas_call(
        functools.partial(kernel, scale, total),
        out_shape=(
            jax.ShapeDtypeStruct((1, 1), F32),
            jax.ShapeDtypeStruct((rows, width), F32),
            jax.ShapeDtypeStruct((rows, width), F32),
        ),
        in_specs=[full] * 3,
        out_specs=(pl.BlockSpec(memory_space=pltpu.SMEM), full, full),
        scratch_shapes=[
            vmem((8, U, width), F32),
            vmem((16, U, width), F32),
            vmem((2, 8 * U, width), BF16),
            vmem((2, width, 8 * U), BF16),
            vmem((2, 16 * U, width), BF16),
            vmem((8 * U, 16 * U), F32),
            vmem((2, 8 * U, 16 * U), BF16),
            vmem((8, U, width), F32),
            vmem((16, width, U), F32),
            vmem((7, U, width), F32),
            vmem((7, width, U), F32),
            vmem((8, width, U), F32),
            vmem((8, U, U), F32),
            vmem((8, U, U), F32),
            vmem((8, 16 * U), F32),
            vmem((8, 16 * U), F32),
            vmem((8, U, U), F32),
            vmem((8, U, U), F32),
            vmem((8, 16 * U), F32),
            vmem((16, U), F32),
            vmem((16, U), F32),
            vmem((9, 16, U), F32),
            vmem((17, 16, U), F32),
            vmem((8, 8, U), F32),
            vmem((16, 8, U), F32),
            vmem((8, U), F32),
            dma((2,)),
            dma((2, 16)),
            dma((1,)),
            dma((8,)),
            dma((8,)),
            dma((2,)),
            dma((2, 14)),
            dma((1,)),
            dma((8,)),
        ],
        compiler_params=pltpu.CompilerParams(
            collective_id=0, has_side_effects=True, vmem_limit_bytes=64 * 1024 * 1024 - 64 * 1024
        ),
    )(pose_emb, text_emb, positive.reshape(1, rows))
    return (loss.reshape(()), pose_grad, text_grad)


def solution(mesh):
    return jax.shard_map(
        per_device,
        mesh=mesh,
        in_specs=(P(("pose", "text"), None), P(("pose", "text"), None), P(("pose", "text"))),
        out_specs=(P(), P(("pose", "text"), None), P(("pose", "text"), None)),
        check_vma=False,
    )
```

```python
import functools
import math

import jax
import jax.numpy as jnp
from jax import lax
from jax.experimental import pallas as pl
from jax.experimental.pallas import tpu as pltpu
from jax.sharding import PartitionSpec as P

F32 = jnp.float32
BF16 = jnp.bfloat16
U = 128
H = U // 2
LOG2E = math.log2(math.e)


def split(v):
    hi = v.astype(BF16)
    return hi, (v - hi.astype(F32)).astype(BF16)


def dot_nn(a, b):
    return jnp.dot(a, b, preferred_element_type=F32)


def dot3(ah, al, bh, bl):
    n = ah.shape[0]
    both = dot_nn(jnp.concatenate([ah, al], axis=0), bh)
    return both[:n] + (both[n:] + dot_nn(ah, bl))


ORDER = [(0, 0), (0, 3), (0, 1), (1, 0), (0, 2), (1, 3), (1, 1), (1, 2)]
SLOT = {place: k for k, place in enumerate(ORDER)}
NXT, PRV, PAR = (0, 1), (0, 3), (1, 0)


def kernel(
    scale,
    total,
    pose_ref,
    text_ref,
    pos_ref,
    loss_ref,
    pg_ref,
    tg_ref,
    xf,
    tf,
    xhl,
    xt,
    thl,
    lg,
    sl,
    gp,
    gt,
    rp,
    rt,
    rsib,
    rm,
    rs,
    cm,
    cs,
    rlt,
    idt,
    cv,
    rowst,
    colst,
    rowrec,
    colrec,
    la,
    lb,
    macc,
    ag_send,
    ag_recv,
    sib_send,
    sib_recv,
    group,
    rs_send,
    rs_recv,
    rsib_send,
    rsib_recv,
):
    width = pose_ref.shape[1]
    pi = lax.axis_index("pose")
    ti = lax.axis_index("text")
    yhi, z, core = pi // 8, (pi // 2) % 4, pi % 2
    ylo, x = ti // 4, ti % 4

    def pabs(dy, dx):
        return (ylo + dy) % 2 * 4 + (x + dx) % 4

    def qabs(dy, dz):
        return (yhi + dy) % 2 * 4 + (z + dz) % 4

    def pose_peer(dy, dx):
        return (pi, pabs(dy, dx))

    def text_peer(dy, dz, dc=0):
        return (qabs(dy, dz) * 2 + (core + dc) % 2, (ylo + dy) % 2 * 4 + x)

    pose_peers = [(dy, dx) for dy in range(2) for dx in range(4) if (dy, dx) != (0, 0)]
    text_peers = [
        (dy, dz, dc)
        for dy in range(2)
        for dz in range(4)
        for dc in range(2)
        if (dy, dz, dc) != (0, 0, 0)
    ]

    barrier = pltpu.get_barrier_semaphore()
    near_by = [pose_peer(*d) for d in (NXT, PRV, PAR)]
    near_by += [text_peer(*d) for d in (NXT, PRV, PAR)] + [text_peer(0, 0, 1)]
    for d in near_by:
        pl.semaphore_signal(barrier, inc=1, device_id=d, device_id_type=pl.DeviceIdType.MESH)
    me_p = pabs(0, 0)
    me_q = pi
    xf[me_p] = pose_ref[...]
    tf[me_q] = text_ref[...]
    pl.semaphore_wait(barrier, len(near_by))

    def copy(src, dst, ssem, rsem, dev):
        c = pltpu.make_async_remote_copy(
            src_ref=src,
            dst_ref=dst,
            send_sem=ssem,
            recv_sem=rsem,
            device_id=dev,
            device_id_type=pl.DeviceIdType.MESH,
        )
        c.start()

    def await_recv(dst, rsem):
        pltpu.make_async_copy(dst, dst, rsem).wait()

    def buf(kind, dy, dd, h):
        if kind == 0:
            return xf.at[pabs(dy, dd), pl.ds(h * H, H)]
        return tf.at[qabs(dy, dd) * 2 + core, pl.ds(h * H, H)]

    def peer(kind, dy, dd):
        return pose_peer(dy, dd) if kind == 0 else text_peer(dy, dd, 0)

    def recv_index(place, h):
        return SLOT[place] * 2 + (h if SLOT[place] < 5 else 0)

    def send(kind, src, h, to, arrives):
        b = buf(kind, *src, h)
        copy(b, b, ag_send.at[kind], ag_recv.at[kind, recv_index(arrives, h)], peer(kind, *to))

    def got(kind, place, h):
        await_recv(buf(kind, *place, h), ag_recv.at[kind, SLOT[place] * 2 + h])

    def whole(kind, dy, dd):
        return xf.at[pabs(dy, dd)] if kind == 0 else tf.at[qabs(dy, dd) * 2 + core]

    def got_whole(kind, place):
        await_recv(whole(kind, *place), ag_recv.at[kind, SLOT[place] * 2])

    def share(place):
        b = whole(1, *place)
        copy(b, b, sib_send.at[0], sib_recv.at[SLOT[place]], text_peer(0, 0, 1))

    def got_sib(place):
        await_recv(tf.at[qabs(*place) * 2 + 1 - core], sib_recv.at[SLOT[place]])

    def rows_of(i, n=1):
        return slice(i * U, (i + n) * U)

    def cols_of(j, n=1):
        return slice(j * 2 * U, (j + n) * 2 * U)

    def convert_pose(i):
        v = xf[pabs(*ORDER[i])]
        xhl[0, rows_of(i), :], xhl[1, rows_of(i), :] = split(v)
        xt[0, :, rows_of(i)], xt[1, :, rows_of(i)] = split(v.T)

    def convert_text(j, dc):
        v = tf[qabs(*ORDER[j]) * 2 + (core + dc) % 2]
        rows = rows_of(2 * j + dc)
        thl[0, rows, :], thl[1, rows, :] = split(v)
        sl[0, 0:width, rows], sl[1, 0:width, rows] = split(v.T)

    def stats(i, v, top, total):
        a, b = v[:, 0:U], v[:, U:]
        old = rm[i]
        new = jnp.maximum(jnp.maximum(a, b), old)
        rs[i] = rs[i] * jnp.exp2(old - new) + jnp.exp2(a - new) + jnp.exp2(b - new)
        rm[i] = new
        w = v.reshape(U // 8, 8, 2 * U)
        new = jnp.maximum(top, jnp.max(w, axis=0))
        return new, total * jnp.exp2(top - new) + jnp.sum(jnp.exp2(w - new[None]), axis=0)

    def logits(i, n, j, count=1):
        def body(jj):
            c = pl.ds(pl.multiple_of(jj * 2 * U, 2 * U), 2 * U)
            th, tl = sl[0, 0:width, c], sl[1, 0:width, c]
            top, total = cm[:, c], cs[:, c]
            k = i
            while k < i + n:
                m = min(2, i + n - k)
                r = rows_of(k, m)
                xh, xl = xhl[0, r, :], xhl[1, r, :]
                v = (scale * LOG2E) * dot3(xh, xl, th, tl)
                lg[r, c] = v
                for q in range(m):
                    top, total = stats(k + q, v[rows_of(q)], top, total)
                k += m
            cm[:, c], cs[:, c] = top, total

        wide = 2 if n <= 2 and count > 1 else 1

        def step(k, carry):
            for u in range(wide):
                body(j + k * wide + u)
            return carry

        if count == 1:
            body(j)
        else:
            lax.fori_loop(0, count // wide, step, 0)
            if count % wide:
                body(j + count - 1)

    for ref in (rm, cm):
        ref[...] = jnp.full_like(ref, -jnp.inf)
    for ref in (rs, cs):
        ref[...] = jnp.zeros_like(ref)

    for h in range(2):
        for kind in range(2):
            send(kind, (0, 0), h, NXT, (0, 3))
            send(kind, (0, 0), 1 - h, PRV, (0, 1))
            send(kind, (0, 0), h, PAR, (1, 0))
    share((0, 0))
    convert_pose(0)
    convert_text(0, 0)

    for kind in range(2):
        got(kind, (0, 3), 0)
        send(kind, (0, 3), 0, NXT, (0, 2))
        got(kind, (0, 1), 1)
        send(kind, (0, 1), 1, PRV, (0, 2))
    for kind in range(2):
        got(kind, (1, 0), 0)
        send(kind, (1, 0), 0, NXT, (1, 3))
        send(kind, (1, 0), 0, PRV, (1, 1))
    got_sib((0, 0))
    convert_text(0, 1)
    for kind in range(2):
        got(kind, (0, 3), 1)
        got(kind, (0, 1), 0)
    for kind in range(2):
        got(kind, (1, 0), 1)
        send(kind, (1, 0), 1, NXT, (1, 3))
        send(kind, (1, 0), 1, PRV, (1, 1))
    for i in (1, 2, 3):
        share(ORDER[i])
    for i in (1, 2, 3):
        convert_pose(i)
        convert_text(i, 0)
    for j in (1, 2, 3):
        got_sib(ORDER[j])
        convert_text(j, 1)
    logits(0, 4, 0, 2)
    for h in range(2):
        for kind in range(2):
            got(kind, (0, 2), h)
            send(kind, (0, 2), h, PAR, (1, 2))
    share((0, 2))
    logits(0, 4, 2, 2)
    convert_pose(4)
    convert_text(4, 0)
    got_sib((0, 2))
    convert_text(4, 1)
    logits(4, 1, 0, 4)
    logits(0, 5, 4)
    for i in (5, 6):
        got_whole(0, ORDER[i])
        convert_pose(i)
    for i in (5, 6):
        got_whole(1, ORDER[i])
        share(ORDER[i])
        convert_text(i, 0)
    logits(5, 2, 0, 5)
    for j in (5, 6):
        got_sib(ORDER[j])
        convert_text(j, 1)
    logits(0, 7, 5, 2)
    for kind in range(2):
        got_whole(kind, (1, 2))
    share((1, 2))
    convert_pose(7)
    convert_text(7, 0)
    logits(7, 1, 0, 7)
    got_sib((1, 2))
    convert_text(7, 1)
    logits(0, 8, 7)

    for i in range(8):
        mt, st = rm[i].T, rs[i].T
        m = jnp.max(mt, axis=0, keepdims=True)
        s = jnp.sum(st * jnp.exp2(mt - m), axis=0, keepdims=True)
        rowst[pl.ds(pabs(*ORDER[i]), 1), :] = m + jnp.log2(s)
    rowst[8:16, :] = jnp.broadcast_to(pos_ref[...].astype(F32), (8, U))
    m = jnp.max(cm[...], axis=0, keepdims=True)
    s = jnp.sum(cs[...] * jnp.exp2(cm[...] - m), axis=0, keepdims=True)
    lse = m + jnp.log2(s)
    for j in range(8):
        for dc in range(2):
            p = qabs(*ORDER[j]) * 2 + (core + dc) % 2
            colst[pl.ds(p, 1), :] = lse[:, rows_of(2 * j + dc)]

    for d in pose_peers:
        copy(rowst, rowrec.at[me_p], group.at[0], group.at[1], pose_peer(*d))
    for d in text_peers:
        copy(colst, colrec.at[me_q], group.at[2], group.at[3], text_peer(*d))
    rowrec[me_p] = rowst[...]
    colrec[me_q] = colst[...]
    await_recv(rowrec.at[0:7], group.at[1])
    await_recv(colrec.at[0:15], group.at[3])

    def lse_of(parts):
        m = parts[0]
        for p in parts[1:]:
            m = jnp.maximum(m, p)
        s = jnp.exp2(parts[0] - m)
        for p in parts[1:]:
            s = s + jnp.exp2(p - m)
        return m + jnp.log2(s)

    rowall, colall = rowrec.at[8], colrec.at[16]
    rowall[0:8] = lse_of([rowrec[k, 0:8, :] for k in range(8)])
    colall[...] = lse_of([colrec[k] for k in range(16)])
    for i in range(8):
        a = pabs(*ORDER[i])
        rlt[i] = jnp.broadcast_to(rowall[pl.ds(a, 1), :] + 1.0, (U, U)).T
        idt[i] = jnp.broadcast_to(rowrec[a, 8:9, :], (U, U)).T

    macc[...] = jnp.zeros_like(macc)
    lane = lax.broadcasted_iota(jnp.int32, (1, U), 1)
    for j, (dy, dz) in enumerate(ORDER):
        for dc in range(2):
            p = qabs(dy, dz) * 2 + (core + dc) % 2
            base = (p * 8 + (ylo + dy) % 2 * 4 + x) * U
            cv[0:1, rows_of(2 * j + dc)] = colall[pl.ds(p, 1), :] + 1.0
            cv[1:2, rows_of(2 * j + dc)] = (base + lane).astype(F32)

    def loop(lo, hi, body):
        def step(k, carry):
            body(k)
            return carry

        if hi > lo:
            lax.fori_loop(lo, hi, step, 0)

    def slope(i2, j):
        acc = None
        for u in range(2):
            rl, ids = rlt[2 * i2 + u], idt[2 * i2 + u]
            r = pl.ds(pl.multiple_of((2 * i2 + u) * U, U), U)
            for dc in range(2):
                c = pl.ds(pl.multiple_of((2 * j + dc) * U, U), U)
                v = lg[r, c]
                hit = ids == cv[1:2, c]
                g = jnp.exp2(v - rl) + jnp.exp2(v - cv[0:1, c])
                t = jnp.where(hit, v, 0.0)
                acc = t if acc is None else acc + t
                hi, lo = split(jnp.where(hit, g - 1.0, g))
                sl[0, r, c] = hi
                sl[1, r, c] = lo
        macc[...] += jnp.sum(acc.reshape(U // 8, 8, U), axis=0)

    reach = {"wide": 8, "tall": 8}

    def slope_for(step, n):
        if step != "T":
            pair = {6: 3, 4: 2, 3: 1, 1: 0}.get(n)
            if pair is not None:
                loop(0, reach["wide"], lambda j: slope(pair, j))
                reach["tall"] = 2 * pair
        else:
            new = min(n, reach["wide"])
            if new < reach["wide"]:
                for j in range(new, reach["wide"]):
                    loop(0, reach["tall"] // 2, lambda i2, j=j: slope(i2, j))
                reach["wide"] = new

    def pose_rows(i, n):
        r = rows_of(i, n)

        def body(k):
            c = pl.ds(pl.multiple_of(k * 2 * U, 2 * U), 2 * U)
            sh, sw = sl[0, r, :], sl[1, r, :]
            th = thl[0, :, c]
            g = dot3(sh, sw, th, thl[1, :, c])
            for u in range(n):
                gp[i + u, :, c] = g[rows_of(u)]

        loop(0, width // (2 * U), body)

    def text_pair(j):
        c = cols_of(j)

        def body(k):
            r = pl.ds(pl.multiple_of(k * 2 * U, 2 * U), 2 * U)
            sh, sw = sl[0, :, c], sl[1, :, c]
            xh = xt[0, r, :]
            g = dot3(xh, xt[1, r, :], sh, sw)
            gt[2 * j, r, :] = g[:, 0:U]
            gt[2 * j + 1, r, :] = g[:, U:]

        loop(0, width // (2 * U), body)
        copy(gt.at[2 * j + 1], rsib.at[j], rsib_send.at[0], rsib_recv.at[j], text_peer(0, 0, 1))

    def g_at(kind, place):
        return gp.at[SLOT[place]] if kind == 0 else gt.at[2 * SLOT[place]]

    def r_at(kind, i):
        return (rp if kind == 0 else rt).at[i]

    def part(ref, h):
        n = ref.shape[0] // 2
        return ref if h is None else ref.at[pl.ds(h * n, n)]

    def rs_index(i, h):
        return i * 2 + (h if i in (0, 3) else 0)

    def rs_send_to(kind, slot, h, to, i):
        copy(
            part(g_at(kind, slot), h),
            part(r_at(kind, i), h),
            rs_send.at[kind],
            rs_recv.at[kind, rs_index(i, h)],
            peer(kind, *to),
        )

    def rs_add(kind, slot, i, h):
        await_recv(part(r_at(kind, i), h), rs_recv.at[kind, rs_index(i, h)])
        dst, src = part(g_at(kind, slot), h), part(r_at(kind, i), h)
        dst[...] += src[...]

    def sib_add(j):
        await_recv(rsib.at[j], rsib_recv.at[j])
        gt[2 * j] += rsib[j]

    def pass_on(step, kind, h):
        if step == "a":
            rs_send_to(kind, (1, 2), h, PAR, 0)
        elif step == "b1":
            rs_send_to(kind, (1, 1), None, NXT, 1)
        elif step == "b2":
            rs_send_to(kind, (1, 3), None, PRV, 2)
        elif step == "c":
            rs_add(kind, (0, 2), 0, h)
            rs_send_to(kind, (0, 2), h, (PRV, NXT)[h], 3)
        elif step == "d":
            rs_add(kind, (1, 0), 1, None)
            rs_add(kind, (1, 0), 2, None)
            rs_send_to(kind, (1, 0), None, PAR, 4)
        else:
            place = (0, 3) if step in ("e0", "f0") else (0, 1)
            if step in ("f0", "f1"):
                rs_add(kind, place, 3, h)
            rs_send_to(kind, place, h, PRV if place == (0, 3) else NXT, 5 if place == (0, 3) else 6)

    def loss_first():
        own = 0.5 * (rowall[pl.ds(me_p, 1), :] + colall[pl.ds(me_q, 1), :])
        first = lax.broadcasted_iota(jnp.int32, (8, U), 0) == 0
        la[me_p] = jnp.where(first, jnp.broadcast_to(own, (8, U)), 0.0) - macc[...]
        b = la.at[me_p]
        for d in pose_peers:
            copy(b, b, group.at[4], group.at[5], pose_peer(*d))

    def loss_second():
        await_recv(la.at[0:7], group.at[5])
        t = la[0]
        for j in range(1, 8):
            t = t + la[j]
        lb[me_q] = t
        b = lb.at[me_q]
        for d in text_peers:
            copy(b, b, group.at[6], group.at[7], text_peer(*d))

    plan = [
        ("T", 7, 0), ("Q", 6, 0), ("a", 0, 0), ("a", 0, 1), ("W", 7, 0), ("a", 1, 0),
        ("a", 1, 1), ("b1", 0, 0), ("Q", 4, 0), ("b2", 0, 0), ("T", 6, 0), ("c", 0, 0),
        ("T", 5, 0), ("W", 6, 0), ("b1", 1, 0), ("T", 4, 0), ("c", 0, 1), ("W", 5, 0),
        ("b2", 1, 0), ("T", 3, 0), ("W", 4, 0), ("c", 1, 0), ("c", 1, 1), ("T", 2, 0),
        ("T", 1, 0), ("W", 2, 0), ("e1", 1, 0), ("P", 3, 0), ("d", 0, 0), ("W", 1, 0),
        ("e0", 1, 1), ("Q", 1, 0), ("L1", 0, 0), ("W", 3, 0), ("d", 1, 0), ("f0", 0, 0),
        ("f1", 0, 1), ("f1", 1, 1), ("e0", 0, 1), ("e1", 0, 0), ("P", 0, 0), ("f0", 1, 0),
        ("T", 0, 0), ("W", 0, 0), ("L2", 0, 0),
    ]
    for step, n, h in plan:
        if step in ("Q", "P"):
            slope_for(step, n)
            pose_rows(n, 2 if step == "Q" else 1)
        elif step == "T":
            slope_for(step, n)
            text_pair(n)
        elif step == "W":
            sib_add(n)
        elif step == "L1":
            loss_first()
        elif step == "L2":
            loss_second()
        else:
            pass_on(step, n, h)

    for i in (4, 5, 6):
        rs_add(0, (0, 0), i, None)
    pg_ref[...] = gp[0]
    await_recv(lb.at[0:15], group.at[7])
    t = lb[0]
    for j in range(1, 16):
        t = t + lb[j]
    loss_ref[0, 0] = jnp.sum(t) / (total * LOG2E)
    for i in (4, 5, 6):
        rs_add(1, (0, 0), i, None)
    tg_ref[...] = gt[0].T

    for kind in range(2):
        await_recv(xf.at[0:7], ag_send.at[kind])
        await_recv(rp, rs_send.at[kind])
    await_recv(xf, sib_send.at[0])
    await_recv(xf, rsib_send.at[0])
    await_recv(rowrec.at[0:7], group.at[0])
    await_recv(colrec.at[0:15], group.at[2])
    await_recv(la.at[0:7], group.at[4])
    await_recv(lb.at[0:15], group.at[6])


def per_device(pose_emb, text_emb, positive):
    rows, width = pose_emb.shape
    total = rows * lax.axis_size("pose") * lax.axis_size("text")
    scale = 2.0 / math.sqrt(width)
    dma = pltpu.SemaphoreType.DMA
    vmem = pltpu.VMEM
    full = pl.BlockSpec(memory_space=pltpu.VMEM)
    loss, pose_grad, text_grad = pl.pallas_call(
        functools.partial(kernel, scale, total),
        out_shape=(
            jax.ShapeDtypeStruct((1, 1), F32),
            jax.ShapeDtypeStruct((rows, width), F32),
            jax.ShapeDtypeStruct((rows, width), F32),
        ),
        in_specs=[full] * 3,
        out_specs=(pl.BlockSpec(memory_space=pltpu.SMEM), full, full),
        scratch_shapes=[
            vmem((8, U, width), F32),
            vmem((16, U, width), F32),
            vmem((2, 8 * U, width), BF16),
            vmem((2, width, 8 * U), BF16),
            vmem((2, 16 * U, width), BF16),
            vmem((8 * U, 16 * U), F32),
            vmem((2, 8 * U, 16 * U), BF16),
            vmem((8, U, width), F32),
            vmem((16, width, U), F32),
            vmem((7, U, width), F32),
            vmem((7, width, U), F32),
            vmem((8, width, U), F32),
            vmem((8, U, U), F32),
            vmem((8, U, U), F32),
            vmem((8, 16 * U), F32),
            vmem((8, 16 * U), F32),
            vmem((8, U, U), F32),
            vmem((8, U, U), F32),
            vmem((8, 16 * U), F32),
            vmem((16, U), F32),
            vmem((16, U), F32),
            vmem((9, 16, U), F32),
            vmem((17, 16, U), F32),
            vmem((8, 8, U), F32),
            vmem((16, 8, U), F32),
            vmem((8, U), F32),
            dma((2,)),
            dma((2, 16)),
            dma((1,)),
            dma((8,)),
            dma((8,)),
            dma((2,)),
            dma((2, 14)),
            dma((1,)),
            dma((8,)),
        ],
        compiler_params=pltpu.CompilerParams(
            collective_id=0, has_side_effects=True, vmem_limit_bytes=64 * 1024 * 1024 - 64 * 1024
        ),
    )(pose_emb, text_emb, positive.reshape(1, rows))
    return (loss.reshape(()), scale * pose_grad, scale * text_grad)


def solution(mesh):
    return jax.shard_map(
        per_device,
        mesh=mesh,
        in_specs=(P(("pose", "text"), None), P(("pose", "text"), None), P(("pose", "text"))),
        out_specs=(P(), P(("pose", "text"), None), P(("pose", "text"), None)),
        check_vma=False,
    )
```
